32 devices in a mesh: dp: 8 (over z, x), noise: 4 (over y, core).
Axes of the slice: x: 2, y: 2, z: 4, core: 2. Of those that a mesh axis runs over, the one named last changes fastest.
Arguments:
- clean_tokens: bfloat16 [32, 64, 1152], P(('dp', 'noise')), may hold values from -6 to 6
- noise_tokens: bfloat16 [4, 32, 64, 1152], P('noise', 'dp'), may hold values from -6 to 6
- time_index: int32 [4, 32], P('noise', 'dp'), may hold values from 0 to 999
- class_label: int32 [32], P(('dp', 'noise')), may hold values from 0 to 999
- velocity_cotangent: bfloat16 [4, 32, 64, 1152], P('noise', 'dp'), may hold values from -6 to 6
- encoder_modulate: bfloat16 [1152, 6912], P('dp', 'noise'), may hold values from -0.1875 to 0.1875
- encoder_attend: bfloat16 [1152, 3456], P('dp', 'noise'), may hold values from -0.1875 to 0.1875
- encoder_merge: bfloat16 [1152, 1152], P('dp', 'noise'), may hold values from -0.375 to 0.375
- encoder_gate: bfloat16 [1152, 3072], P('dp', 'noise'), may hold values from -0.1875 to 0.1875
- encoder_lift: bfloat16 [1152, 3072], P('dp', 'noise'), may hold values from -0.1875 to 0.1875
- encoder_lower: bfloat16 [3072, 1152], P('dp', 'noise'), may hold values from -0.109375 to 0.109375
- class_table: bfloat16 [1152, 1000], P('dp', 'noise'), may hold values from -6 to 6
- encoder_gains: float32 [2, 72], replicated, may hold values from 0.25 to 1.75
- decoder_modulate: bfloat16 [1152, 6912], P('dp', 'noise'), may hold values from -0.1875 to 0.1875
- decoder_attend: bfloat16 [1152, 3456], P('dp', 'noise'), may hold values from -0.1875 to 0.1875
- decoder_merge: bfloat16 [1152, 1152], P('dp', 'noise'), may hold values from -0.375 to 0.375
- decoder_gate: bfloat16 [1152, 3072], P('dp', 'noise'), may hold values from -0.1875 to 0.1875
- decoder_lift: bfloat16 [1152, 3072], P('dp', 'noise'), may hold values from -0.1875 to 0.1875
- decoder_lower: bfloat16 [3072, 1152], P('dp', 'noise'), may hold values from -0.109375 to 0.109375
- time_weight: bfloat16 [1152, 1152], P('dp', 'noise'), may hold values from -0.1875 to 0.1875
- decoder_gains: float32 [2, 72], replicated, may hold values from 0.25 to 1.75
Outputs:
- velocity: bfloat16 [4, 32, 64, 1152], P('noise', 'dp')
- latent_tokens: bfloat16 [32, 64, 1152], P(('dp', 'noise'))
- clean_grad: float32 [32, 64, 1152], P(('dp', 'noise'))
- grad_encoder_modulate: float32 [1152, 6912], P('dp', 'noise')
- grad_encoder_attend: float32 [1152, 3456], P('dp', 'noise')
- grad_encoder_merge: float32 [1152, 1152], P('dp', 'noise')
- grad_encoder_gate: float32 [1152, 3072], P('dp', 'noise')
- grad_encoder_lift: float32 [1152, 3072], P('dp', 'noise')
- grad_encoder_lower: float32 [3072, 1152], P('dp', 'noise')
- grad_class_table: float32 [1152, 1000], P('dp', 'noise')
- grad_encoder_gains: float32 [2, 72], replicated
- grad_decoder_modulate: float32 [1152, 6912], P('dp', 'noise')
- grad_decoder_attend: float32 [1152, 3456], P('dp', 'noise')
- grad_decoder_merge: float32 [1152, 1152], P('dp', 'noise')
- grad_decoder_gate: float32 [1152, 3072], P('dp', 'noise')
- grad_decoder_lift: float32 [1152, 3072], P('dp', 'noise')
- grad_decoder_lower: float32 [3072, 1152], P('dp', 'noise')
- grad_time_weight: float32 [1152, 1152], P('dp', 'noise')
- grad_decoder_gains: float32 [2, 72], replicated
The draws below stay inside these ranges and needn't reach their ends.
All inputs are finite; a program needn't handle non-finite values.
Results may differ from the reference program's by a relative error of at most 0.035.
Values may be sent and summed in bfloat16 or wider, within the bound.
No kernel may reach another device: no remote copies, remote signals or barrier semaphores. Data moves between devices by JAX's collectives and lax.ppermute only.
A program may use at most 512 MiB of HBM per device.

```python
import math
import jax
import jax.numpy as jnp
from jax import lax

D = 1152
HEADS = 16
HEAD = 72
FF = 3072
CLASSES = 1000
NT = 1000
GRID = 8
IMG_DEV = 4
SEQ = 64
LEVELS = 4
IMAGES = 32


def with_ends(entries, own_key, least, top_value):
    spot = [jax.random.randint(jax.random.fold_in(own_key, axis), (), 0, length) for axis, length in enumerate(entries.shape)]
    main_axis = entries.shape.index(max(entries.shape))
    next_to = spot[:main_axis] + [(spot[main_axis] + 1) % entries.shape[main_axis]] + spot[main_axis + 1:]
    return entries.at[tuple(spot)].set(least).at[tuple(next_to)].set(top_value)


def shard_levels(stream_key, shape, shards, least, high):
    def one(dim, shards_of):
        heights = jax.random.uniform(jax.random.fold_in(jax.random.fold_in(stream_key, 6), dim), (shards_of,), jnp.float32, least / len(shards), high / len(shards))
        return jnp.repeat(jnp.exp(heights), shape[dim] // shards_of).reshape((-1,) + (1,) * (len(shape) - dim - 1))

    factor_of = one(*shards[0])
    for cut in shards[1:]:
        factor_of = factor_of * one(*cut)
    return factor_of


def scatter_about(own_key, dims, scale, limit, cuts=(), held_as=jnp.bfloat16):
    array = scale * jax.random.normal(own_key, dims, jnp.float32)
    if cuts:
        array = array * shard_levels(own_key, dims, cuts, -0.22, 0.18)
    return jnp.clip(array, -limit, limit).astype(held_as)


def setup_inputs(seed: int = 0) -> dict:
    seeds = jax.random.split(jax.random.key(seed), 22)
    clean_tokens = scatter_about(seeds[0], (IMAGES, SEQ, D), 1.0, 6.0, ((0, 32),))
    noise_tokens = scatter_about(seeds[1], (LEVELS, IMAGES, SEQ, D), 1.0, 6.0, ((0, 4), (1, 8)))
    time_index = with_ends(jax.random.randint(seeds[2], (LEVELS, IMAGES), 0, NT), jax.random.fold_in(seeds[2], 1), 0, NT - 1).astype(jnp.int32)
    class_label = with_ends(jax.random.randint(seeds[3], (IMAGES,), 0, CLASSES), jax.random.fold_in(seeds[3], 1), 0, CLASSES - 1).astype(jnp.int32)
    velocity_cotangent = scatter_about(seeds[4], (LEVELS, IMAGES, SEQ, D), 1.0, 6.0, ((0, 4), (1, 8)))
    encoder_modulate = scatter_about(seeds[5], (D, 6 * D), D ** -0.5, 0.1875, ((0, 8), (1, 4)))
    encoder_attend = scatter_about(seeds[6], (D, 3 * D), D ** -0.5, 0.1875, ((0, 8), (1, 4)))
    encoder_merge = scatter_about(seeds[7], (D, D), (D // 4) ** -0.5, 0.375, ((0, 8), (1, 4)))
    encoder_gate = scatter_about(seeds[8], (D, FF), D ** -0.5, 0.1875, ((0, 8), (1, 4)))
    encoder_lift = scatter_about(seeds[9], (D, FF), D ** -0.5, 0.1875, ((0, 8), (1, 4)))
    encoder_lower = scatter_about(seeds[10], (FF, D), FF ** -0.5, 0.109375, ((0, 8), (1, 4)))
    class_table = scatter_about(seeds[11], (D, CLASSES), 1.0, 6.0, ((0, 8), (1, 4)))
    encoder_gains = jnp.clip(1.0 + 0.15 * jax.random.normal(seeds[12], (2, HEAD), jnp.float32), 0.25, 1.75)
    decoder_modulate = scatter_about(seeds[13], (D, 6 * D), D ** -0.5, 0.1875, ((0, 8), (1, 4)))
    decoder_attend = scatter_about(seeds[14], (D, 3 * D), D ** -0.5, 0.1875, ((0, 8), (1, 4)))
    decoder_merge = scatter_about(seeds[15], (D, D), (D // 4) ** -0.5, 0.375, ((0, 8), (1, 4)))
    decoder_gate = scatter_about(seeds[16], (D, FF), D ** -0.5, 0.1875, ((0, 8), (1, 4)))
    decoder_lift = scatter_about(seeds[17], (D, FF), D ** -0.5, 0.1875, ((0, 8), (1, 4)))
    decoder_lower = scatter_about(seeds[18], (FF, D), FF ** -0.5, 0.109375, ((0, 8), (1, 4)))
    time_weight = scatter_about(seeds[19], (D, D), D ** -0.5, 0.1875, ((0, 8), (1, 4)))
    decoder_gains = jnp.clip(1.0 + 0.15 * jax.random.normal(seeds[20], (2, HEAD), jnp.float32), 0.25, 1.75)
    return {"clean_tokens": clean_tokens, "noise_tokens": noise_tokens, "time_index": time_index, "class_label": class_label, "velocity_cotangent": velocity_cotangent, "encoder_modulate": encoder_modulate, "encoder_attend": encoder_attend, "encoder_merge": encoder_merge, "encoder_gate": encoder_gate, "encoder_lift": encoder_lift, "encoder_lower": encoder_lower, "class_table": class_table, "encoder_gains": encoder_gains, "decoder_modulate": decoder_modulate, "decoder_attend": decoder_attend, "decoder_merge": decoder_merge, "decoder_gate": decoder_gate, "decoder_lift": decoder_lift, "decoder_lower": decoder_lower, "time_weight": time_weight, "decoder_gains": decoder_gains}


EPS = 1e-06

@jax.custom_vjp
def low(v):
    return lax.optimization_barrier(v.astype(jnp.bfloat16)).astype(jnp.float32)

@jax.custom_vjp
def low_back(v):
    return v

def low_keep(v):
    return (low(v), None)

def low_pass(kept, grad):
    return (grad,)

def back_keep(v):
    return (v, None)

def back_low(kept, grad):
    return (low(grad),)
low.defvjp(low_keep, low_pass)
low_back.defvjp(back_keep, back_low)

def layer_norm(value):
    center = value - lax.optimization_barrier(jnp.mean(value, -1, keepdims=True))
    return center * lax.rsqrt(lax.optimization_barrier(jnp.mean(center * center, -1, keepdims=True)) + EPS)

def rms_norm(value, scale_gain):
    return value * lax.rsqrt(lax.optimization_barrier(jnp.mean(value * value, -1, keepdims=True)) + EPS) * scale_gain

def angle_tables(length):
    places = jnp.arange(length)
    quarter = HEAD // 4
    freqs = jnp.exp(-math.log(10000.0) * jnp.arange(quarter).astype(jnp.float32) / quarter)
    row_angle = (places // GRID).astype(jnp.float32)[:, None] * freqs[None, :]
    col_angle = (places % GRID).astype(jnp.float32)[:, None] * freqs[None, :]
    return (row_angle, col_angle)

def turn_half(value, angle):
    quarter = angle.shape[-1]
    cosine = jnp.cos(angle)[:, None, :]
    sine = jnp.sin(angle)[:, None, :]
    first = value[..., :quarter]
    second = value[..., quarter:]
    return jnp.concatenate([first * cosine - second * sine, second * cosine + first * sine], -1)

def rotate(value):
    row_angle, col_angle = angle_tables(value.shape[1])
    half = value.shape[-1] // 2
    return jnp.concatenate([turn_half(value[..., :half], row_angle), turn_half(value[..., half:], col_angle)], -1)

def head_norms(project, gains):
    count, length, triple = project.shape
    width = triple // 3
    shape = (count, length, HEADS, width // HEADS)
    queries = rotate(rms_norm(project[..., :width].reshape(shape), gains[0]))
    keys_head = rotate(rms_norm(project[..., width:2 * width].reshape(shape), gains[1]))
    values = project[..., 2 * width:].reshape(shape)
    return (queries, keys_head, values)

def sinusoid(times, width):
    half = width // 2
    freqs = jnp.exp(-math.log(10000.0) * jnp.arange(half).astype(jnp.float32) / half)
    angle = (times * 1000.0)[..., None] * freqs
    return jnp.concatenate([jnp.cos(angle), jnp.sin(angle)], -1)

def block_ref(hidden, cond, weights, gains):
    precise = lax.Precision.HIGHEST
    w_mod, w_att, w_merge, w_gate, w_lift, w_lower = weights
    count, length, width = hidden.shape
    silu_cond = low(jax.nn.silu(cond))
    modulate = low_back(jnp.einsum('nsd,df->nsf', silu_cond, w_mod, precision=precise))
    shift_one, scale_one, gate_one, shift_two, scale_two, gate_two = jnp.split(modulate, 6, axis=-1)
    normed_one = low(layer_norm(hidden) * (1.0 + scale_one) + shift_one)
    project = low_back(jnp.einsum('nsd,df->nsf', normed_one, w_att, precision=precise))
    queries, keys_head, values = head_norms(project, gains)
    queries = low(queries)
    keys_head = low(keys_head)
    values = low(values)
    scores = low_back(jnp.einsum('nqhe,nkhe->nhqk', queries, keys_head, precision=precise) * HEAD ** (-0.5))
    attn_prob = low(jax.nn.softmax(scores, axis=-1))
    mixed = low_back(low(jnp.einsum('nhqk,nkhe->nqhe', attn_prob, values, precision=precise))).reshape(count, length, width)
    merged = low_back(jnp.einsum('nsd,df->nsf', mixed, w_merge, precision=precise))
    middle = hidden + gate_one * merged
    normed_two = low(layer_norm(middle) * (1.0 + scale_two) + shift_two)
    gate_act = low_back(jnp.einsum('nsd,df->nsf', normed_two, w_gate, precision=precise))
    lift_act = low_back(jnp.einsum('nsd,df->nsf', normed_two, w_lift, precision=precise))
    hidden_act = low(jax.nn.silu(gate_act) * lift_act)
    lowered = low_back(jnp.einsum('nsf,fd->nsd', hidden_act, w_lower, precision=precise))
    return middle + gate_two * lowered

def reference(clean_tokens, noise_tokens, time_index, class_label, velocity_cotangent, encoder_modulate, encoder_attend, encoder_merge, encoder_gate, encoder_lift, encoder_lower, class_table, encoder_gains, decoder_modulate, decoder_attend, decoder_merge, decoder_gate, decoder_lift, decoder_lower, time_weight, decoder_gains):
    precise = lax.Precision.HIGHEST
    groups = IMAGES // IMG_DEV
    noise_all = jnp.moveaxis(noise_tokens.astype(jnp.float32).reshape(LEVELS, groups, IMG_DEV, SEQ, D), 1, 0)
    times_all = jnp.moveaxis(((time_index.astype(jnp.float32) + 0.5) / NT).reshape(LEVELS, groups, IMG_DEV), 1, 0)
    labels_all = class_label.reshape(groups, IMG_DEV)
    params = (clean_tokens, encoder_modulate, encoder_attend, encoder_merge, encoder_gate, encoder_lift, encoder_lower, class_table, encoder_gains, decoder_modulate, decoder_attend, decoder_merge, decoder_gate, decoder_lift, decoder_lower, time_weight, decoder_gains)
    params = tuple((p.astype(jnp.float32) for p in params))

    def forward(clean, e_mod, e_att, e_merge, e_gate, e_lift, e_lower, table, e_gains, d_mod, d_att, d_merge, d_gate, d_lift, d_lower, t_weight, d_gains):
        enc_weights = (e_mod, e_att, e_merge, e_gate, e_lift, e_lower)
        dec_weights = (d_mod, d_att, d_merge, d_gate, d_lift, d_lower)

        def image_group(clean_group, noise_group, times_group, label_group):
            class_cond = jnp.take(table, label_group, axis=1).T[:, None, :]
            latent = low(block_ref(clean_group, class_cond, enc_weights, e_gains))
            sines = low(sinusoid(times_group, D))
            temb = low_back(jnp.einsum('lgd,df->lgf', sines, t_weight, precision=precise))
            cond = latent[None] + temb[:, :, None, :]
            ratio = times_group[:, :, None, None]
            noisy = (1.0 - ratio) * clean_group[None] + ratio * noise_group
            out = block_ref(noisy.reshape(-1, SEQ, D), cond.reshape(-1, SEQ, D), dec_weights, d_gains)
            return (out.reshape(LEVELS, IMG_DEV, SEQ, D), latent)
        checked = jax.checkpoint(image_group)

        def scan_step(carried, batch_item):
            return (carried, checked(*batch_item))
        _, (velocities, latents) = lax.scan(scan_step, jnp.zeros((), jnp.float32), (clean.reshape(groups, IMG_DEV, SEQ, D), noise_all, times_all, labels_all))
        velocities = jnp.moveaxis(velocities, 0, 1).reshape(LEVELS, IMAGES, SEQ, D)
        return (velocities, latents.reshape(IMAGES, SEQ, D))
    (velocities, latents), pullback = jax.vjp(forward, *params)
    grads = pullback((velocity_cotangent.astype(jnp.float32), jnp.zeros_like(latents)))
    return (velocities.astype(jnp.bfloat16), latents.astype(jnp.bfloat16), grads[0], grads[1], grads[2], grads[3], grads[4], grads[5], grads[6], grads[7], grads[8], grads[9], grads[10], grads[11], grads[12], grads[13], grads[14], grads[15], grads[16])
```

```python
import functools
import math

import jax
import jax.numpy as jnp
import numpy as np
from jax import lax
from jax.experimental import pallas as pl
from jax.experimental.pallas import tpu as pltpu
from jax.sharding import PartitionSpec as P

HEADS = 16
HEAD = 72
NT = 1000
GRID = 8


EPS = 1e-06


def angle_tables(length):
    places = jnp.arange(length)
    quarter = HEAD // 4
    freqs = jnp.exp(-math.log(10000.0) * jnp.arange(quarter).astype(jnp.float32) / quarter)
    row_angle = (places // GRID).astype(jnp.float32)[:, None] * freqs[None, :]
    col_angle = (places % GRID).astype(jnp.float32)[:, None] * freqs[None, :]
    return (row_angle, col_angle)


def sinusoid(times, width):
    half = width // 2
    freqs = jnp.exp(-math.log(10000.0) * jnp.arange(half).astype(jnp.float32) / half)
    angle = (times * 1000.0)[..., None] * freqs
    return jnp.concatenate([jnp.cos(angle), jnp.sin(angle)], -1)


BF = jnp.bfloat16
F32 = jnp.float32


def dot(left, right):
    return jnp.dot(left, right, preferred_element_type=F32)


def dot_nt(left, right):
    return lax.dot_general(left, right, (((1,), (1,)), ((), ())), preferred_element_type=F32)


def dot_tn(left, right):
    return lax.dot_general(left, right, (((0,), (0,)), ((), ())), preferred_element_type=F32)


def dot_tt(left, right):
    return lax.dot_general(left, right, (((0,), (1,)), ((), ())), preferred_element_type=F32)


def pick(array, index, axis=0):
    return lax.dynamic_index_in_dim(array, index, axis, keepdims=False)


class Noise:
    def __init__(self, count):
        self.count = count
        self.me = lax.axis_index("noise")
        self.quick = count == 4

    def swap(self, array, mask):
        return lax.ppermute(array, "noise", [(n, n ^ mask) for n in range(self.count)])

    def order(self, near):
        odd = self.me % 2 == 1
        far = self.me // 2 == 1
        near = [
            jnp.where(odd, near[1], near[0]),
            jnp.where(odd, near[0], near[1]),
            jnp.where(odd, near[3], near[2]),
            jnp.where(odd, near[2], near[3]),
        ]
        return [
            jnp.where(far, near[2], near[0]),
            jnp.where(far, near[3], near[1]),
            jnp.where(far, near[0], near[2]),
            jnp.where(far, near[1], near[3]),
        ]

    def gather(self, array):
        if not self.quick:
            whole = lax.all_gather(array, "noise", axis=0, tiled=False)
            return [whole[n] for n in range(self.count)]
        across = self.swap(array, 2)
        beside = self.swap(array, 1)
        corner = self.swap(across, 1)
        return self.order([array, beside, across, corner])

    def near(self, array):
        across = self.swap(array, 2)
        beside = self.swap(array, 1)
        return [array, beside, across, self.swap(across, 1)]

    def near_sum(self, keep, send):
        half = keep.astype(F32) + self.swap(send, 1).astype(F32)
        return half[0] + self.swap(half[1].astype(BF), 2).astype(F32)

    def scatter_sum(self, blocks, wire=BF):
        if not self.quick:
            return lax.psum_scatter(
                blocks.astype(wire), "noise", scatter_dimension=0, tiled=False
            ).astype(F32)
        core = self.me % 2
        far = self.me // 2
        pairs = blocks.reshape((2, 2) + blocks.shape[1:])
        keep = pick(pairs, core, 1).astype(F32)
        send = pick(pairs, 1 - core, 1).astype(wire)
        half = keep + self.swap(send, 1).astype(F32)
        return pick(half, far) + self.swap(pick(half, 1 - far).astype(wire), 2).astype(F32)

    def total(self, array):
        if not self.quick:
            return lax.psum(array, "noise")
        array = array + self.swap(array, 1)
        return array + self.swap(array, 2)

    def exchange(self, blocks):
        if not self.quick:
            whole = lax.all_to_all(blocks, "noise", 0, 0)
            return [whole[n] for n in range(self.count)]
        near = [pick(blocks, self.me)]
        for mask in (1, 2, 3):
            near.append(self.swap(pick(blocks, self.me ^ mask), mask))
        return self.order(near)


class Groups:
    def __init__(self, count):
        self.count = count
        self.quick = count == 8
        self.sides = 2
        self.line = count // 2
        self.place = lax.axis_index("dp")
        self.spot = self.place // self.sides
        self.side = self.place % self.sides
        self.across = [
            (z * 2 + x, z * 2 + 1 - x) for z in range(self.line) for x in range(2)
        ]

    def shift(self, array, spots, step):
        pairs = [(z * 2 + x, (z + step) * 2 + x) for z in spots for x in range(2)]
        return lax.ppermute(array, "dp", pairs)

    def swap(self, array, mask):
        return lax.ppermute(array, "dp", [(n, n ^ mask) for n in range(self.count)])

    def gather_whole(self, array):
        return lax.all_gather(array, "dp", axis=0, tiled=False)

    def sum_whole(self, blocks):
        return lax.psum_scatter(
            blocks.astype(BF), "dp", scatter_dimension=0, tiled=False
        ).astype(F32)

    def gather(self, array):
        if not self.quick:
            return self.gather_whole(array)
        last = self.line - 1
        lower, upper = [], []
        up = down = array
        for step in range(1, self.line):
            up = self.shift(up, range(step - 1, last), 1)
            down = self.shift(down, range(1, self.line - step + 1), -1)
            lower.append(up)
            upper.append(down)
        stack = jnp.stack(lower[::-1] + [array] + upper)
        own = lax.dynamic_slice_in_dim(stack, last - self.spot, self.line, 0)
        other = lax.ppermute(own, "dp", self.across)
        first = jnp.where(self.side == 0, own, other)
        second = jnp.where(self.side == 0, other, own)
        whole = jnp.stack([first, second], 1)
        return whole.reshape((self.count,) + array.shape)

    def scatter_sum(self, blocks, wire=BF):
        if not self.quick:
            return self.sum_whole(blocks)
        last = self.line - 1
        pairs = blocks.reshape((self.line, 2) + blocks.shape[1:])
        keep = pick(pairs, self.side, 1).astype(F32)
        send = pick(pairs, 1 - self.side, 1).astype(wire)
        half = keep + lax.ppermute(send, "dp", self.across).astype(F32)
        up = down = None
        for step in range(1, self.line):
            ahead = pick(half, jnp.minimum(self.spot + self.line - step, last))
            behind = pick(half, jnp.maximum(self.spot - self.line + step, 0))
            if up is not None:
                ahead = ahead + up
                behind = behind + down
            up = self.shift(ahead.astype(wire), range(0, step), 1).astype(F32)
            down = self.shift(
                behind.astype(wire), range(self.line - step, self.line), -1
            ).astype(F32)
        return pick(half, self.spot) + up + down

    def gather_small(self, array):
        if not self.quick:
            return self.gather_whole(array)
        array = array[None]
        for mask in (1, 2, 4):
            other = self.swap(array, mask)
            high = (self.place // mask) % 2 == 1
            array = jnp.where(
                high, jnp.concatenate([other, array]), jnp.concatenate([array, other])
            )
        return array

    def sum_small(self, blocks):
        if not self.quick:
            return lax.psum_scatter(blocks, "dp", scatter_dimension=0, tiled=False)
        for mask in (4, 2, 1):
            halves = blocks.reshape((2, -1) + blocks.shape[1:])
            high = (self.place // mask) % 2
            blocks = pick(halves, high) + self.swap(pick(halves, 1 - high), mask)
        return blocks[0]

    def total(self, array):
        if not self.quick:
            return lax.psum(array, "dp")
        for mask in (1, 2, 4):
            array = array + self.swap(array, mask)
        return array


def split_pieces(noise, weight, pieces):
    count = noise.count
    rows, width = weight.shape
    chunk = width // pieces
    slots = -(-pieces // count)
    parts = jnp.moveaxis(weight.reshape(rows, pieces, chunk), 1, 0)
    parts = jnp.concatenate(
        [parts, jnp.zeros((slots * count - pieces, rows, chunk), weight.dtype)]
    ).reshape(slots, count, rows, chunk)
    parts = jnp.roll(parts, pieces * noise.me, axis=1)
    return jnp.moveaxis(parts, 1, 0)


def take_pieces(noise, came, pieces):
    count = noise.count
    out = []
    for piece in range(pieces):
        chunk = count * piece + noise.me
        out.append(came[chunk // pieces, (chunk % pieces) // count])
    return jnp.stack(out, 1)


def return_pieces(noise, grad):
    count = noise.count
    pieces = grad.shape[1]
    slots = -(-pieces // count)
    rows = []
    for target in range(count):
        first = (noise.me - pieces * target) % count
        line = []
        for slot in range(slots):
            turn = jnp.minimum(first + slot * count, pieces - 1)
            line.append(pick(grad, (pieces * target + turn) // count, 1))
        rows.append(jnp.stack(line))
    return jnp.stack(rows)


def join_pieces(noise, came, pieces):
    count = noise.count
    out = []
    for turn in range(pieces):
        chunk = pieces * noise.me + turn
        out.append(came[chunk % count, turn // count])
    joined = jnp.stack(out, 1)
    return joined.reshape(joined.shape[0], -1)


def split_units(noise, groups, weight):
    count = noise.count
    rows, width = weight.shape
    low = groups.count // count
    parts = weight.reshape(rows, low, count, width // (low * count))
    return parts.transpose(2, 0, 1, 3).reshape(count, rows, width // count)


def take_units(noise, groups, came):
    count, rows, width = came.shape
    return jnp.moveaxis(came, 0, 1).reshape(rows, count * width)


def return_units(noise, grad):
    rows, width = grad.shape
    return jnp.moveaxis(grad.reshape(rows, noise.count, width // noise.count), 1, 0)


def join_units(noise, groups, came):
    count, rows, width = came.shape
    low = groups.count // count
    parts = came.reshape(count, rows, low, width // low)
    return parts.transpose(1, 2, 0, 3).reshape(rows, count * width)


def place_weights(noise, groups, w_att, w_gate, w_lift, w_lower, w_mod=None):
    rows = w_att.shape[0]
    att = split_pieces(noise, w_att, 3)
    chunk = att.shape[-1]
    parts = [att.reshape(noise.count, rows, chunk)]
    if w_mod is not None:
        mod = split_pieces(noise, w_mod, 6)
        parts += [mod[:, 0], mod[:, 1]]
    parts.append(split_units(noise, groups, w_gate))
    parts.append(split_units(noise, groups, w_lift))
    unit = parts[-1].shape[-1]
    parts.append(w_lower.reshape(noise.count, rows, unit))
    came = jnp.stack(noise.exchange(jnp.concatenate(parts, -1)))
    spot = 0
    out = [take_pieces(noise, came[:, None, :, :chunk], 3)]
    spot = chunk
    if w_mod is not None:
        mod = jnp.stack([came[:, :, chunk : 2 * chunk], came[:, :, 2 * chunk : 3 * chunk]], 1)
        out.append(take_pieces(noise, mod, 6))
        spot = 3 * chunk
    out.append(take_units(noise, groups, came[:, :, spot : spot + unit]))
    spot += unit
    out.append(take_units(noise, groups, came[:, :, spot : spot + unit]))
    spot += unit
    lower = came[:, :, spot:].reshape(noise.count, -1, w_lower.shape[1])
    lower = jnp.moveaxis(lower, 0, 1)
    out.append(lower.reshape(lower.shape[0], -1))
    return out


def flat(weight):
    return weight.reshape(weight.shape[0] * weight.shape[1], -1)


def norm_parts(value):
    mean = jnp.mean(value, -1, keepdims=True)
    center = value - mean
    inverse = lax.rsqrt(jnp.mean(center * center, -1, keepdims=True) + EPS)
    return center * inverse, inverse


def norm_back(grad, normed, inverse):
    first = jnp.mean(grad, -1, keepdims=True)
    second = jnp.mean(grad * normed, -1, keepdims=True)
    return inverse * (grad - first - normed * second)


def silu_slope(value):
    gate = jax.nn.sigmoid(value)
    return gate * (1.0 + value * (1.0 - gate))


VMEM_BYTES = 48 * 1024 * 1024
STEP = 256


def kernel_call(kernel, grid, ins, outs, scratch=(), scalars=1):
    return pl.pallas_call(
        kernel,
        out_shape=[shape for shape, _ in outs],
        grid_spec=pltpu.PrefetchScalarGridSpec(
            num_scalar_prefetch=scalars,
            grid=grid,
            in_specs=ins,
            out_specs=[spec for _, spec in outs],
            scratch_shapes=list(scratch),
        ),
        compiler_params=pltpu.CompilerParams(vmem_limit_bytes=VMEM_BYTES),
    )


def row_spec(width):
    return pl.BlockSpec((STEP, width), lambda n, *_: (n, 0))


def up_spec(width):
    return pl.BlockSpec((width, STEP), lambda n, *_: (0, n))


def full_spec(shape):
    return pl.BlockSpec(shape, lambda n, *_: (0,) * len(shape))


def shaped(shape, dtype):
    return jax.ShapeDtypeStruct(shape, dtype)


def joined(me_ref, near, parts):
    for n, ref in enumerate(near):
        parts[me_ref[0] ^ n] = ref[...]
    return jnp.concatenate([parts[n] for n in range(4)])


def near_scratch(near):
    return [pltpu.VMEM((4, near[0].shape[0], STEP), BF)]


def join_kernel(upward, me_ref, x0, x1, x2, x3, w_ref, full_ref, out_ref, parts):
    whole = joined(me_ref, (x0, x1, x2, x3), parts)
    full_ref[...] = whole
    if upward:
        out_ref[...] = dot_tn(w_ref[...], whole)
    else:
        out_ref[...] = dot_tn(whole, w_ref[...])


def join_dot(me, near, weight, upward=False):
    quarter, rows = near[0].shape
    width = weight.shape[1]
    if upward:
        out = (shaped((width, rows), F32), up_spec(width))
    else:
        out = (shaped((rows, width), F32), row_spec(width))
    return kernel_call(
        functools.partial(join_kernel, upward),
        (rows // STEP,),
        [up_spec(quarter)] * 4 + [full_spec(weight.shape)],
        [(shaped((4 * quarter, rows), BF), up_spec(4 * quarter)), out],
        near_scratch(near),
    )(me, *near, weight)


def units_kernel(me_ref, x0, x1, x2, x3, w_ref, full_ref, out_ref, hid_ref, parts):
    whole = joined(me_ref, (x0, x1, x2, x3), parts)
    full_ref[...] = whole
    acts = dot_tn(whole, w_ref[...])
    out_ref[...] = acts
    unit = hid_ref.shape[1]
    hid_ref[...] = (jax.nn.silu(acts[:, :unit]) * acts[:, unit:]).astype(BF)


def units_dot(me, near, weight):
    quarter, rows = near[0].shape
    width = weight.shape[1]
    return kernel_call(
        units_kernel,
        (rows // STEP,),
        [up_spec(quarter)] * 4 + [full_spec(weight.shape)],
        [
            (shaped((4 * quarter, rows), BF), up_spec(4 * quarter)),
            (shaped((rows, width), F32), row_spec(width)),
            (shaped((rows, width // 2), BF), row_spec(width // 2)),
        ],
        near_scratch(near),
    )(me, *near, weight)


def lower_kernel(me_ref, x0, x1, x2, x3, w_ref, full_ref, out_ref, parts):
    whole = joined(me_ref, (x0, x1, x2, x3), parts).T
    full_ref[...] = whole
    out_ref[...] = dot_nt(whole, w_ref[...])


def lower_back_dot(me, near, weight):
    quarter, rows = near[0].shape
    width = weight.shape[0]
    return kernel_call(
        lower_kernel,
        (rows // STEP,),
        [up_spec(quarter)] * 4 + [full_spec(weight.shape)],
        [
            (shaped((rows, 4 * quarter), BF), row_spec(4 * quarter)),
            (shaped((rows, width), F32), row_spec(width)),
        ],
        near_scratch(near),
    )(me, *near, weight)


def give(parts, keep_ref, send_ref):
    keep_ref[0] = parts[0]
    keep_ref[1] = parts[2]
    send_ref[0] = parts[1]
    send_ref[1] = parts[3]


def give_outs(rows, quarter):
    pair = pl.BlockSpec((2, quarter, STEP), lambda n, *_: (0, 0, n))
    return [(shaped((2, quarter, rows), BF), pair)] * 2


def spread_kernel(me_ref, y_ref, w_ref, keep_ref, send_ref, parts):
    quarter = keep_ref.shape[1]
    value = y_ref[...]
    for n in range(4):
        term = dot_nt(w_ref[n * quarter : (n + 1) * quarter], value)
        parts[me_ref[0] ^ n] = term.astype(BF)
    give(parts, keep_ref, send_ref)


def spread_dot(me, value, weight):
    rows, width = value.shape
    quarter = weight.shape[0] // 4
    return kernel_call(
        spread_kernel,
        (rows // STEP,),
        [row_spec(width), full_spec(weight.shape)],
        give_outs(rows, quarter),
        [pltpu.VMEM((4, quarter, STEP), BF)],
    )(me, value, weight)


def spread_up_kernel(me_ref, y_ref, w_ref, keep_ref, send_ref, parts):
    quarter = keep_ref.shape[1]
    value = y_ref[...]
    for n in range(4):
        term = dot(w_ref[n * quarter : (n + 1) * quarter], value)
        parts[me_ref[0] ^ n] = term.astype(BF)
    give(parts, keep_ref, send_ref)


def spread_up_dot(me, value, weight):
    width, rows = value.shape
    quarter = weight.shape[0] // 4
    return kernel_call(
        spread_up_kernel,
        (rows // STEP,),
        [up_spec(width), full_spec(weight.shape)],
        give_outs(rows, quarter),
        [pltpu.VMEM((4, quarter, STEP), BF)],
    )(me, value, weight)


def lowered_kernel(me_ref, y_ref, w_ref, keep_ref, send_ref, parts):
    quarter = keep_ref.shape[1]
    term = dot(y_ref[...], w_ref[...]).astype(BF).T
    for n in range(4):
        parts[me_ref[0] ^ n] = term[n * quarter : (n + 1) * quarter]
    give(parts, keep_ref, send_ref)


def lowered_dot(me, value, weight):
    rows, width = value.shape
    quarter = weight.shape[1] // 4
    return kernel_call(
        lowered_kernel,
        (rows // STEP,),
        [row_spec(width), full_spec(weight.shape)],
        give_outs(rows, quarter),
        [pltpu.VMEM((4, quarter, STEP), BF)],
    )(me, value, weight)


def acts_back_kernel(me_ref, g_ref, a_ref, w_ref, acts_ref, keep_ref, send_ref, parts):
    quarter = keep_ref.shape[1]
    unit = g_ref.shape[1]
    grad = g_ref[...]
    gate_act, lift_act = a_ref[:, :unit], a_ref[:, unit:]
    gate = jax.nn.sigmoid(gate_act)
    slope = gate * (1.0 + gate_act * (1.0 - gate))
    acts_ref[:, :unit] = (grad * lift_act * slope).astype(BF)
    acts_ref[:, unit:] = (grad * (gate_act * gate)).astype(BF)
    value = acts_ref[...]
    for n in range(4):
        term = dot_nt(w_ref[n * quarter : (n + 1) * quarter], value)
        parts[me_ref[0] ^ n] = term.astype(BF)
    give(parts, keep_ref, send_ref)


def acts_back(me, grad, acts, weight):
    rows, unit = grad.shape
    quarter = weight.shape[0] // 4
    return kernel_call(
        acts_back_kernel,
        (rows // STEP,),
        [row_spec(unit), row_spec(2 * unit), full_spec(weight.shape)],
        [(shaped((rows, 2 * unit), BF), row_spec(2 * unit))] + give_outs(rows, quarter),
        [pltpu.VMEM((4, quarter, STEP), BF)],
    )(me, grad, acts, weight)


def grad_kernel(x_ref, y_ref, out_ref):
    out_ref[...] = dot(x_ref[...], y_ref[...]).astype(BF)


def grad_turned_kernel(x_ref, y_ref, out_ref):
    out_ref[...] = dot_nt(x_ref[...], y_ref[...]).astype(BF)


def grad_low_kernel(x_ref, y_ref, out_ref):
    out_ref[...] = dot_tn(x_ref[...], y_ref[...]).astype(BF)


def grad_dot(left, right, kernel=grad_kernel):
    step = 384
    low = kernel is grad_low_kernel
    width, rows = left.shape[::-1] if low else left.shape
    wide = right.shape[0] if kernel is grad_turned_kernel else right.shape[1]
    if low:
        spec = pl.BlockSpec((rows, step), lambda n: (0, n))
    else:
        spec = pl.BlockSpec((step, rows), lambda n: (n, 0))
    return pl.pallas_call(
        kernel,
        out_shape=shaped((width, wide), BF),
        grid=(width // step,),
        in_specs=[spec, pl.BlockSpec(right.shape, lambda n: (0, 0))],
        out_specs=pl.BlockSpec((step, wide), lambda n: (n, 0)),
        compiler_params=pltpu.CompilerParams(vmem_limit_bytes=VMEM_BYTES),
    )(left, right)


def mod_kernel(x_ref, w_ref, out_ref):
    out_ref[...] = dot(x_ref[...], w_ref[...]).T


def mod_dot(value, weight):
    rows, width = value.shape
    wide = weight.shape[1]
    return kernel_call(
        mod_kernel,
        (rows // STEP,),
        [row_spec(width), full_spec(weight.shape)],
        [(shaped((wide, rows), F32), up_spec(wide))],
        scalars=0,
    )(value, weight)[0]


def mod_back_kernel(*refs):
    parts, (w_ref, cat_ref, out_ref) = refs[:6], refs[6:]
    grad = jnp.concatenate([ref[...] for ref in parts]).T
    cat_ref[...] = grad
    out_ref[...] = dot_nt(grad, w_ref[...])


def mod_back(parts, weight):
    quarter, rows = parts[0].shape
    return kernel_call(
        mod_back_kernel,
        (rows // STEP,),
        [up_spec(quarter)] * 6 + [full_spec(weight.shape)],
        [
            (shaped((rows, 6 * quarter), BF), row_spec(6 * quarter)),
            (shaped((rows, weight.shape[0]), F32), row_spec(weight.shape[0])),
        ],
        scalars=0,
    )(*parts, weight)


def kind_width(kind, quarter):
    if kind[0] == "pieces":
        return -(-kind[1] // 4) * quarter
    if kind[0] == "units":
        return kind[1] // 4
    return quarter


def pack_parts(me, kinds, low, quarter):
    out = []
    spot = 0
    for item, kind in enumerate(kinds):
        for far in range(4):
            to = me ^ far
            if kind[0] == "pieces":
                count = kind[1]
                for slot in range(-(-count // 4)):
                    turn = (to - count * me) % 4 + 4 * slot
                    if turn < count:
                        out.append(
                            (item, far, None, turn * quarter, spot + slot * quarter, quarter)
                        )
            elif kind[0] == "units":
                each = kind[1] // (4 * low)
                for n in range(low):
                    at = n * 4 * each + to * each
                    out.append((item, far, None, at, spot + n * each, each))
            else:
                out.append((item, far, (to * kind[1], kind[1]), 0, spot, quarter))
        spot += kind_width(kind, quarter)
    return out


def unpack_parts(me, kinds, low, quarter):
    out = []
    spot = 0
    for item, kind in enumerate(kinds):
        for far in range(4):
            come = me ^ far
            if kind[0] == "pieces":
                count = kind[1]
                for slot in range(-(-count // 4)):
                    turn = (me - count * come) % 4 + 4 * slot
                    if turn < count:
                        piece = (count * come + turn) // 4
                        out.append(
                            (item, far, None, piece * quarter, spot + slot * quarter, quarter)
                        )
            elif kind[0] == "units":
                each = kind[1] // (4 * low)
                for n in range(low):
                    at = (come * low + n) * each
                    out.append((item, far, None, at, spot + n * each, each))
            else:
                out.append((item, far, (0, kind[1]), come * quarter, spot, quarter))
        spot += kind_width(kind, quarter)
    return out


def pack_kernel(plan, me_ref, *refs):
    items, out_ref = refs[:-1], refs[-1]
    out_ref[...] = jnp.zeros_like(out_ref)
    for me in range(4):

        @pl.when(me_ref[0] == me)
        def _():
            for item, far, lines, at, spot, size in plan(me):
                first, count = lines or (0, out_ref.shape[1])
                out_ref[far, :count, spot : spot + size] = items[item][
                    first : first + count, at : at + size
                ].astype(BF)


def unpack_kernel(plan, me_ref, *refs):
    packets, outs = refs[:4], refs[4:]
    for me in range(4):

        @pl.when(me_ref[0] == me)
        def _():
            for item, far, lines, at, spot, size in plan(me):
                first, count = lines or (0, packets[0].shape[0])
                outs[item][first : first + count, at : at + size] = packets[far][
                    :count, spot : spot + size
                ].astype(outs[item].dtype)


def whole_call(kernel, outs, me, args):
    return kernel_call(
        kernel,
        (1,),
        [full_spec(arg.shape) for arg in args],
        [(out, full_spec(out.shape)) for out in outs],
    )(me, *args)


def trade(noise, me, arrays, kinds, low, back, shapes, dtype):
    quarter = kind_quarter(kinds, arrays, back)
    width = sum(kind_width(kind, quarter) for kind in kinds)
    lines = max(a.shape[0] for a, kind in zip(arrays, kinds) if kind[0] != "lower")
    there, here = (unpack_parts, pack_parts) if back else (pack_parts, unpack_parts)
    packed = whole_call(
        functools.partial(
            pack_kernel, functools.partial(there, kinds=kinds, low=low, quarter=quarter)
        ),
        [shaped((4, lines, width), BF)],
        me,
        arrays,
    )[0]
    near = [packed[0]] + [noise.swap(packed[n], n) for n in (1, 2, 3)]
    return whole_call(
        functools.partial(
            unpack_kernel, functools.partial(here, kinds=kinds, low=low, quarter=quarter)
        ),
        [shaped(shape, dtype) for shape in shapes],
        me,
        near,
    )


def kind_quarter(kinds, arrays, back):
    for array, kind in zip(arrays, kinds):
        if kind[0] == "pieces":
            return array.shape[1] // kind[1]
        if kind[0] == "lower":
            return array.shape[1] // 4 if back else array.shape[1]


def attend_tables(length, repeat, gains):
    heads = HEADS // 4
    row_angle, col_angle = angle_tables(length)
    angle = jnp.concatenate([row_angle, row_angle, col_angle, col_angle], -1)
    angle = jnp.tile(angle, (repeat, heads))
    spread = jnp.tile(gains, (1, heads))
    return jnp.cos(angle), jnp.sin(angle), spread


def attend_matrices():
    width = HEADS // 4 * HEAD
    quarter = HEAD // 4
    index = np.arange(width)
    same = (index[:, None] // HEAD == index[None, :] // HEAD).astype(np.float32)
    second = (index % (2 * quarter)) >= quarter
    source = np.where(second, index - quarter, index + quarter)
    turn = np.zeros((width, width), np.float32)
    turn[source, index] = np.where(second, 1.0, -1.0)
    low = jnp.asarray(same, BF), jnp.asarray(turn, BF), jnp.asarray(turn.T, BF)
    return low


def halves_dot(value, matrix):
    high = value.astype(BF)
    rest = (value - high.astype(F32)).astype(BF)
    return dot(high, matrix) + dot(rest, matrix)


def head_masks(width):
    lane = lax.broadcasted_iota(jnp.int32, (1, width), 1)
    return [
        jnp.logical_and(lane >= n * HEAD, lane < (n + 1) * HEAD).astype(F32)
        for n in range(width // HEAD)
    ]


def ready_heads(value, gain, cosine, sine, same, turn):
    inverse = lax.rsqrt(halves_dot(value * value, same) * (1.0 / HEAD) + EPS)
    normed = value * inverse
    scaled = normed * gain
    turned = scaled * cosine + halves_dot(scaled, turn) * sine
    return turned.astype(BF), normed, inverse


def stack_heads(value, masks):
    value = value.astype(F32)
    return jnp.concatenate([value * mask for mask in masks]).astype(BF)


def fold_heads(value, masks, length):
    out = value[:length] * masks[0]
    for n in range(1, len(masks)):
        out = out + value[n * length : (n + 1) * length] * masks[n]
    return out


def prob_of(stacked, keys_low):
    scores = dot_nt(stacked, keys_low) * HEAD ** (-0.5)
    grown = jnp.exp(scores - jnp.max(scores, -1, keepdims=True))
    return grown / jnp.sum(grown, -1, keepdims=True)


def attend_kernel(
    length,
    upward,
    p_ref,
    cos_ref,
    sin_ref,
    gain_ref,
    same_ref,
    turn_ref,
    out_ref,
    mixed_ref,
):
    width = mixed_ref.shape[1]
    q_ref, k_ref, v_ref = [p_ref[:, n * width : (n + 1) * width] for n in range(3)]
    masks = head_masks(width)
    same, turn = same_ref[...], turn_ref[...]
    cosine, sine = cos_ref[...], sin_ref[...]
    query, _, _ = ready_heads(q_ref, gain_ref[0:1], cosine, sine, same, turn)
    key, _, _ = ready_heads(k_ref, gain_ref[1:2], cosine, sine, same, turn)
    value = v_ref.astype(BF)
    for image in range(mixed_ref.shape[0] // length):
        part = slice(image * length, (image + 1) * length)
        prob = prob_of(stack_heads(query[part], masks), key[part])
        mixed = dot(prob.astype(BF), value[part])
        mixed_ref[part] = fold_heads(mixed, masks, length)
    if upward:
        out_ref[...] = mixed_ref[...].T.astype(BF)
    else:
        out_ref[...] = mixed_ref[...].astype(BF)


def attend_back_kernel(
    length,
    upward,
    p_ref,
    cos_ref,
    sin_ref,
    gain_ref,
    same_ref,
    turn_ref,
    back_ref,
    grad_ref,
    dp_ref,
    dg_ref,
    gq_ref,
    gk_ref,
    gv_ref,
):
    width = gq_ref.shape[1]
    q_ref, k_ref, v_ref = [p_ref[:, n * width : (n + 1) * width] for n in range(3)]
    masks = head_masks(width)
    same, turn, back = same_ref[...], turn_ref[...], back_ref[...]
    cosine, sine = cos_ref[...], sin_ref[...]
    query, q_norm, q_inv = ready_heads(q_ref, gain_ref[0:1], cosine, sine, same, turn)
    key, k_norm, k_inv = ready_heads(k_ref, gain_ref[1:2], cosine, sine, same, turn)
    value = v_ref.astype(BF)
    grad = grad_ref[...].T if upward else grad_ref[...]
    for image in range(q_ref.shape[0] // length):
        part = slice(image * length, (image + 1) * length)
        stacked = stack_heads(query[part], masks)
        prob = prob_of(stacked, key[part])
        grads = stack_heads(grad[part], masks)
        gv_ref[part] = dot_tn(prob.astype(BF), grads)
        g_prob = dot_nt(grads, value[part])
        g_score = prob * (g_prob - jnp.sum(g_prob * prob, -1, keepdims=True))
        g_score = g_score.astype(BF)
        gq_ref[part] = fold_heads(dot(g_score, key[part]), masks, length)
        gk_ref[part] = dot_tn(g_score, stacked)

    @pl.when(pl.program_id(0) == 0)
    def _():
        dg_ref[...] = jnp.zeros_like(dg_ref)

    for n, (g_ref, normed, inverse) in enumerate(
        ((gq_ref, q_norm, q_inv), (gk_ref, k_norm, k_inv))
    ):
        turned = g_ref[...] * HEAD ** (-0.5)
        scaled = turned * cosine + halves_dot(turned * sine, back)
        dg_ref[n : n + 1] += jnp.sum(scaled * normed, 0, keepdims=True)
        weighed = scaled * gain_ref[n : n + 1]
        mean = halves_dot(weighed * normed, same) * (1.0 / HEAD)
        out = inverse * (weighed - normed * mean)
        dp_ref[:, n * width : (n + 1) * width] = out.astype(BF)
    dp_ref[:, 2 * width :] = gv_ref[...].astype(BF)


def attend_blocks(rows, length, width):
    step = STEP

    def row(size):
        return pl.BlockSpec((step, size), lambda n: (n, 0))

    def whole(*shape):
        return pl.BlockSpec(shape, lambda n: (0, 0))

    return step, row, whole


def attend_forward(project, gains, length, upward=False):
    rows, width = project.shape[0], project.shape[1] // 3
    step, row, whole = attend_blocks(rows, length, width)
    cosine, sine, spread = attend_tables(length, step // length, gains)
    same, turn, _ = attend_matrices()
    return pl.pallas_call(
        functools.partial(attend_kernel, length, upward),
        out_shape=shaped((width, rows) if upward else (rows, width), BF),
        grid=(rows // step,),
        in_specs=[row(3 * width), whole(step, width), whole(step, width), whole(2, width)]
        + [whole(width, width)] * 2,
        out_specs=up_spec(width) if upward else row(width),
        scratch_shapes=[pltpu.VMEM((step, width), F32)],
        compiler_params=pltpu.CompilerParams(vmem_limit_bytes=VMEM_BYTES),
    )(project, cosine, sine, spread, same, turn)


def attend_backward(grad_low, gains, project, length, upward=False):
    rows, width = project.shape[0], project.shape[1] // 3
    step, row, whole = attend_blocks(rows, length, width)
    cosine, sine, spread = attend_tables(length, step // length, gains)
    same, turn, back = attend_matrices()
    grad, gain_grad = pl.pallas_call(
        functools.partial(attend_back_kernel, length, upward),
        out_shape=(shaped((rows, 3 * width), BF), shaped((2, width), F32)),
        grid=(rows // step,),
        in_specs=[row(3 * width), whole(step, width), whole(step, width), whole(2, width)]
        + [whole(width, width)] * 3
        + [up_spec(width) if upward else row(width)],
        out_specs=(row(3 * width), whole(2, width)),
        scratch_shapes=[pltpu.VMEM((step, width), F32)] * 3,
        compiler_params=pltpu.CompilerParams(vmem_limit_bytes=VMEM_BYTES),
    )(project, cosine, sine, spread, same, turn, back, grad_low)
    return grad, jnp.sum(gain_grad.reshape(2, width // HEAD, HEAD), 1)


def per_device(
    groups_count,
    noise_count,
    clean_tokens,
    noise_tokens,
    time_index,
    class_label,
    velocity_cotangent,
    encoder_modulate,
    encoder_attend,
    encoder_merge,
    encoder_gate,
    encoder_lift,
    encoder_lower,
    class_table,
    encoder_gains,
    decoder_modulate,
    decoder_attend,
    decoder_merge,
    decoder_gate,
    decoder_lift,
    decoder_lower,
    time_weight,
    decoder_gains,
):
    noise = Noise(noise_count)
    groups = Groups(groups_count)
    own_images, length, width = clean_tokens.shape
    images = own_images * noise_count
    levels = noise_count
    quarter = width // noise_count
    own_rows = own_images * length
    rows = images * length
    place = noise.me * quarter

    def columns(value):
        return lax.dynamic_slice_in_dim(value, place, quarter, value.ndim - 1)

    def column_blocks(value):
        return jnp.moveaxis(value.reshape(value.shape[0], noise_count, quarter), 1, 0)

    def token_blocks(value):
        return value.reshape(noise_count, own_rows, width)

    me = noise.me.reshape(1)
    unit = encoder_gate.shape[1]
    chunk_rows = encoder_attend.shape[0]
    lower_rows = encoder_lower.shape[0] // noise_count
    low_units = groups_count // noise_count
    e_kinds = (("pieces", 3), ("units", unit), ("units", unit), ("lower", lower_rows))
    d_kinds = e_kinds + (("pieces", 6),)
    shapes = ((chunk_rows, 3 * quarter), (chunk_rows, unit), (chunk_rows, unit))
    shapes += ((lower_rows, width), (chunk_rows, 6 * quarter))
    if groups.quick:
        e_att_s, e_gate_s, e_lift_s, e_lower_s = trade(
            noise,
            me,
            (encoder_attend, encoder_gate, encoder_lift, encoder_lower),
            e_kinds,
            low_units,
            False,
            shapes[:4],
            BF,
        )
    else:
        e_att_s, e_gate_s, e_lift_s, e_lower_s = place_weights(
            noise, groups, encoder_attend, encoder_gate, encoder_lift, encoder_lower
        )
    (
        e_att_s,
        e_gate_s,
        e_lift_s,
        e_lower_s,
        clean_tokens,
        noise_tokens,
        velocity_cotangent,
        time_index,
        class_label,
        decoder_attend,
        decoder_gate,
    ) = lax.optimization_barrier(
        (
            e_att_s,
            e_gate_s,
            e_lift_s,
            e_lower_s,
            clean_tokens,
            noise_tokens,
            velocity_cotangent,
            time_index,
            class_label,
            decoder_attend,
            decoder_gate,
        )
    )
    e_first = groups.gather(
        jnp.concatenate([e_att_s.reshape(chunk_rows, -1), encoder_merge], -1)
    )
    e_att = flat(e_first[:, :, : 3 * quarter])
    e_merge = flat(e_first[:, :, 3 * quarter :])
    e_second = groups.gather(jnp.concatenate([e_gate_s, e_lift_s], -1))
    e_gate = flat(e_second[:, :, :unit])
    e_lift = flat(e_second[:, :, unit:])
    e_lower = flat(groups.gather(e_lower_s))
    if groups.quick:
        d_att_s, d_gate_s, d_lift_s, d_lower_s, d_mod_s = trade(
            noise,
            me,
            (decoder_attend, decoder_gate, decoder_lift, decoder_lower, decoder_modulate),
            d_kinds,
            low_units,
            False,
            shapes,
            BF,
        )
    else:
        d_att_s, d_mod_s, d_gate_s, d_lift_s, d_lower_s = place_weights(
            noise,
            groups,
            decoder_attend,
            decoder_gate,
            decoder_lift,
            decoder_lower,
            decoder_modulate,
        )
    d_first_s = jnp.concatenate(
        [
            d_mod_s.reshape(chunk_rows, -1),
            d_att_s.reshape(chunk_rows, -1),
            decoder_merge,
            time_weight,
        ],
        -1,
    )

    def pad_lower(part):
        ends = ((0, 0),) * (part.ndim - 1) + ((0, 2 * unit - width),)
        return jnp.pad(part, ends)

    d_second_s = jnp.concatenate(
        [jnp.concatenate([d_gate_s, d_lift_s], -1), pad_lower(d_lower_s)]
    )
    d_first_s, _ = lax.optimization_barrier((d_first_s, e_second))
    d_whole = flat(groups.gather_whole(d_first_s))
    d_second_s, d_whole = lax.optimization_barrier((d_second_s, d_whole))
    d_pair = groups.gather_whole(d_second_s)
    d_mod, d_att, d_merge, d_time = [
        d_whole[:, first * quarter : last * quarter]
        for first, last in ((0, 6), (6, 9), (9, 10), (10, 11))
    ]
    d_units = flat(d_pair[:, :chunk_rows])
    d_lower = flat(d_pair[:, chunk_rows:, :width])

    facts = jnp.concatenate([class_label, time_index[0]])
    facts = jnp.stack(noise.gather(facts))
    times = (facts[:, own_images:].astype(F32) + 0.5) / NT
    labels = groups.gather_small(facts[:, :own_images].reshape(-1)).reshape(-1)

    here = class_table.shape[1]
    onehot = (
        labels[:, None] == (jnp.arange(here) + noise.me * here)[None, :]
    ).astype(BF)
    class_cond = noise.total(dot_nt(onehot, class_table))
    class_low = jax.nn.silu(class_cond).astype(BF)
    class_mod = dot(class_low, encoder_modulate)
    class_mod = groups.sum_small(
        class_mod.reshape(groups_count, images, class_mod.shape[1])
    )
    class_mod = jnp.concatenate(noise.gather(class_mod), -1)

    clean_group = jnp.concatenate(noise.gather(clean_tokens.reshape(own_rows, width)))
    clean_all = clean_group.astype(F32)
    own_times = (time_index[0].astype(F32) + 0.5) / NT
    own_ratio = jnp.repeat(own_times, length)[:, None]
    own_noise = noise_tokens[0].reshape(rows, width)
    own_cot = velocity_cotangent[0].reshape(rows, width)
    own_noisy = (1.0 - own_ratio) * clean_all + own_ratio * own_noise.astype(F32)
    own_mean = jnp.mean(own_noisy, -1)
    own_center = own_noisy - own_mean[:, None]
    own_inverse = lax.rsqrt(jnp.mean(own_center * own_center, -1) + EPS)
    stats = jnp.stack(noise.gather(jnp.stack([own_mean, own_inverse])))
    mean_one = stats[:, 0].reshape(1, -1)
    inverse_one = stats[:, 1].reshape(1, -1)
    came = noise.exchange(
        jnp.stack(
            [
                own_noise.T.reshape(noise_count, quarter, rows),
                own_cot.T.reshape(noise_count, quarter, rows),
            ],
            1,
        )
    )
    noise_cols = jnp.concatenate([part[0] for part in came], -1)
    cot_cols = jnp.concatenate([part[1] for part in came], -1).astype(F32)

    e_piece = [
        jnp.repeat(part, length, axis=0) for part in jnp.split(class_mod, 6, axis=-1)
    ]
    e_norm_one, e_inverse_one = norm_parts(clean_all)
    e_one = (e_norm_one * (1.0 + e_piece[1]) + e_piece[0]).astype(BF)
    e_heads = dot(e_one, e_att)
    e_mixed = attend_forward(e_heads, encoder_gains, length)
    e_mixed_all = jnp.concatenate(noise.gather(e_mixed), -1)
    e_merged = jnp.concatenate(
        noise.gather(dot(e_mixed_all, e_merge).astype(BF)), -1
    ).astype(F32)
    e_middle = clean_all + e_piece[2] * e_merged
    e_norm_two, e_inverse_two = norm_parts(e_middle)
    e_two = (e_norm_two * (1.0 + e_piece[4]) + e_piece[3]).astype(BF)
    e_gate_act = dot(e_two, e_gate)
    e_lift_act = dot(e_two, e_lift)
    e_hidden = (jax.nn.silu(e_gate_act) * e_lift_act).astype(BF)
    e_lowered = noise.scatter_sum(token_blocks(dot(e_hidden, e_lower)))

    def own_part(value):
        return lax.dynamic_slice_in_dim(value, noise.me * own_rows, own_rows, 0)

    latent_own = own_part(e_middle) + own_part(e_piece[5]) * e_lowered
    latent_low = latent_own.astype(BF)
    latent_all = jnp.concatenate(noise.gather(latent_low)).astype(F32)

    sines = sinusoid(times, width).astype(BF).reshape(levels * images, width)
    temb = jnp.concatenate(noise.gather(dot(sines, d_time)), -1)
    cond = (
        latent_all.reshape(1, images, length, width)
        + temb.reshape(levels, images, 1, width)
    ).reshape(levels * rows, width)
    cond_low = jax.nn.silu(cond).astype(BF)
    mod = mod_dot(cond_low, d_mod)
    shift_one, scale_one, gate_one, shift_two, scale_two, gate_two = [
        mod[n * quarter : (n + 1) * quarter] for n in range(6)
    ]
    ratio = jnp.repeat(times.reshape(-1), length)[None]
    clean_up = lax.dynamic_slice_in_dim(clean_group.T, place, quarter, 0).astype(F32)
    noisy = (1.0 - ratio) * jnp.tile(clean_up, (1, levels)) + ratio * noise_cols.astype(F32)
    norm_one = (noisy - mean_one) * inverse_one
    one = (norm_one * (1.0 + scale_one) + shift_one).astype(BF)
    one_all, heads = join_dot(me, noise.near(one), d_att)
    mixed = attend_forward(heads, decoder_gains, length, True)
    mixed_all, merged = join_dot(me, noise.near(mixed), d_merge, True)
    middle = noisy + gate_one * merged
    part_mean = jnp.mean(middle, 0)
    part_center = middle - part_mean[None]
    part_square = jnp.sum(part_center * part_center, 0)
    parts = noise.near(jnp.stack([part_mean, part_square]))
    mean_two = sum(part[0] for part in parts) / noise_count
    square = sum(part[1] + quarter * (part[0] - mean_two) ** 2 for part in parts)
    inverse_two = lax.rsqrt(square / width + EPS)[None]
    norm_two = (middle - mean_two[None]) * inverse_two
    two = (norm_two * (1.0 + scale_two) + shift_two).astype(BF)
    two_all, acts, hidden = units_dot(me, noise.near(two), d_units)
    lowered = noise.near_sum(*lowered_dot(me, hidden, d_lower))
    output = (middle + gate_two * lowered).astype(BF)
    velocity = jnp.concatenate(
        noise.exchange(jnp.moveaxis(output.reshape(quarter, levels, rows), 1, 0))
    )
    velocity = velocity.T.reshape(1, images, length, width)

    def norm_back_cols(grad, normed, inverse):
        sums = noise.total(jnp.stack([jnp.sum(grad, 0), jnp.sum(grad * normed, 0)]))
        sums = sums[:, None] / width
        return inverse * (grad - sums[0] - normed * sums[1])

    low_cols = (cot_cols * gate_two).astype(BF)
    low_all, g_hidden = lower_back_dot(me, noise.near(low_cols), d_lower)
    g_gate_two = cot_cols * lowered
    g_acts, *given = acts_back(me, g_hidden, acts, d_units)
    g_two = noise.near_sum(*given)
    gw_lower = grad_dot(hidden, low_all, grad_low_kernel)
    gw_units = grad_dot(two_all, g_acts)
    g_middle = cot_cols + norm_back_cols(g_two * (1.0 + scale_two), norm_two, inverse_two)
    g_merged_low = (g_middle * gate_one).astype(BF)
    g_mixed = noise.near_sum(*spread_up_dot(me, g_merged_low, d_merge))
    gw_merge = grad_dot(mixed_all, g_merged_low, grad_turned_kernel)
    g_heads, d_gain_grad = attend_backward(
        g_mixed.astype(BF), decoder_gains, heads, length, True
    )
    g_one = noise.near_sum(*spread_dot(me, g_heads, d_att))
    gw_att = grad_dot(one_all, g_heads)
    g_noisy = g_middle + norm_back_cols(g_one * (1.0 + scale_one), norm_one, inverse_one)
    g_parts = (
        g_one,
        g_one * norm_one,
        g_middle * merged,
        g_two,
        g_two * norm_two,
        g_gate_two,
    )
    g_mod, g_cond_low = mod_back([part.astype(BF) for part in g_parts], d_mod)
    gw_mod = grad_dot(cond_low, g_mod, grad_low_kernel)
    g_cond = g_cond_low * silu_slope(cond)
    g_temb = noise.scatter_sum(
        column_blocks(jnp.sum(g_cond.reshape(levels * images, length, width), 1)), F32
    ).astype(BF)
    gw_time = dot_tn(sines, g_temb)
    g_latent = noise.scatter_sum(token_blocks(jnp.sum(g_cond.reshape(levels, rows, width), 0)))
    g_clean_cols = jnp.sum(
        ((1.0 - ratio) * g_noisy).reshape(quarter, levels, rows), 1
    ).astype(BF).T
    g_clean = jnp.concatenate(
        noise.exchange(g_clean_cols.reshape(noise_count, own_rows, quarter)), -1
    ).astype(F32)

    piece = [own_part(part) for part in e_piece]
    norm_two_own = own_part(e_norm_two)
    norm_one_own = own_part(e_norm_one)
    e_low_all = jnp.concatenate(noise.gather((g_latent * piece[5]).astype(BF)))
    e_g_gate_two = g_latent * e_lowered
    ew_lower = dot_tn(e_hidden, e_low_all)
    e_g_hidden = dot_nt(e_low_all, e_lower)
    e_g_gate_low = (e_g_hidden * e_lift_act * silu_slope(e_gate_act)).astype(BF)
    e_g_lift_low = (e_g_hidden * jax.nn.silu(e_gate_act)).astype(BF)
    ew_gate = dot_tn(e_two, e_g_gate_low)
    ew_lift = dot_tn(e_two, e_g_lift_low)
    e_g_two = noise.scatter_sum(
        token_blocks(dot_nt(e_g_gate_low, e_gate) + dot_nt(e_g_lift_low, e_lift))
    )
    e_g_middle = g_latent + norm_back(
        e_g_two * (1.0 + piece[4]), norm_two_own, own_part(e_inverse_two)
    )
    e_merged_low = jnp.concatenate(noise.gather((e_g_middle * piece[2]).astype(BF)))
    e_merged_cols = columns(e_merged_low)
    ew_merge = dot_tn(e_mixed_all, e_merged_cols)
    e_g_mixed = noise.scatter_sum(column_blocks(dot_nt(e_merged_cols, e_merge)))
    e_g_heads, e_gain_grad = attend_backward(
        e_g_mixed.astype(BF), encoder_gains, e_heads, length
    )
    ew_att = dot_tn(e_one, e_g_heads)
    e_g_one = noise.scatter_sum(token_blocks(dot_nt(e_g_heads, e_att)))
    e_g_clean = e_g_middle + norm_back(
        e_g_one * (1.0 + piece[1]), norm_one_own, own_part(e_inverse_one)
    )
    clean_grad = (e_g_clean + g_clean).reshape(own_images, length, width)
    e_g_mod = jnp.concatenate(
        [
            e_g_one,
            e_g_one * norm_one_own,
            e_g_middle * own_part(e_merged),
            e_g_two,
            e_g_two * norm_two_own,
            e_g_gate_two,
        ],
        -1,
    )
    e_g_mod = jnp.sum(e_g_mod.reshape(own_images, length, -1), 1).astype(BF)
    every_mod = noise.exchange(
        jnp.moveaxis(e_g_mod.reshape(own_images, noise_count, -1), 1, 0)
    )
    every_mod = groups.gather_small(jnp.concatenate(every_mod))
    every_mod = every_mod.reshape(-1, every_mod.shape[-1])
    grad_e_mod = dot_tn(class_low, every_mod)
    g_class = noise.total(dot_nt(every_mod, encoder_modulate)) * silu_slope(class_cond)
    grad_table = lax.dot_general(
        g_class,
        onehot.astype(F32),
        (((0,), (0,)), ((), ())),
        precision=lax.Precision.HIGHEST,
        preferred_element_type=F32,
    )

    def by_group(grad):
        low = grad.astype(BF)
        return low.reshape((groups_count, -1) + low.shape[1:])

    def finish_pieces(mine, pieces):
        mine = mine.astype(BF).reshape(mine.shape[0], pieces, quarter)
        came = jnp.stack(noise.exchange(return_pieces(noise, mine)))
        return join_pieces(noise, came, pieces).astype(F32)

    def finish_units(mine):
        came = jnp.stack(noise.exchange(return_units(noise, mine.astype(BF))))
        return join_units(noise, groups, came).astype(F32)

    def finish_lower(mine):
        mine = mine.astype(BF).reshape(-1, width)
        came = jnp.stack(noise.exchange(column_blocks(mine)))
        return came.reshape(-1, quarter).astype(F32)

    def finish(arrays, picked, e_or_d):
        kinds = tuple(e_or_d[n] for n in picked)
        full = (
            (chunk_rows, encoder_attend.shape[1]),
            (chunk_rows, unit),
            (chunk_rows, unit),
            encoder_lower.shape,
            (chunk_rows, encoder_modulate.shape[1]),
        )
        if groups.quick:
            return trade(
                noise,
                me,
                arrays,
                kinds,
                low_units,
                True,
                [full[n] for n in picked],
                F32,
            )
        ends = {"units": finish_units, "lower": finish_lower}
        return [
            finish_pieces(array, kind[1]) if kind[0] == "pieces" else ends[kind[0]](array)
            for array, kind in zip(arrays, kinds)
        ]

    d_second = groups.sum_whole(
        jnp.concatenate([by_group(gw_units), pad_lower(by_group(gw_lower))], 1)
    )
    grad_d_gate, grad_d_lift, grad_d_lower = finish(
        (
            d_second[:chunk_rows, :unit],
            d_second[:chunk_rows, unit:],
            d_second[chunk_rows:, :width],
        ),
        (1, 2, 3),
        d_kinds,
    )
    d_first = groups.sum_whole(
        jnp.concatenate([by_group(part) for part in [gw_mod, gw_att, gw_merge, gw_time]], -1)
    )
    grad_d_att, grad_d_mod = finish(
        (d_first[:, 6 * quarter : 9 * quarter], d_first[:, : 6 * quarter]), (0, 4), d_kinds
    )
    grad_d_merge = d_first[:, 9 * quarter : 10 * quarter]
    grad_time = d_first[:, 10 * quarter :]
    e_low_sum = groups.scatter_sum(by_group(ew_lower))
    e_second = groups.scatter_sum(
        jnp.concatenate([by_group(ew_gate), by_group(ew_lift)], -1)
    )
    e_first = groups.scatter_sum(
        jnp.concatenate([by_group(part) for part in [ew_att, ew_merge]], -1)
    )
    grad_e_att, grad_e_gate, grad_e_lift, grad_e_lower = finish(
        (e_first[:, : 3 * quarter], e_second[:, :unit], e_second[:, unit:], e_low_sum),
        (0, 1, 2, 3),
        e_kinds,
    )
    grad_e_merge = e_first[:, 3 * quarter :]
    gain_total = groups.total(noise.total(jnp.stack([e_gain_grad, d_gain_grad])))
    return (
        velocity,
        latent_low.reshape(own_images, length, width),
        clean_grad,
        grad_e_mod,
        grad_e_att,
        grad_e_merge,
        grad_e_gate,
        grad_e_lift,
        grad_e_lower,
        grad_table,
        gain_total[0],
        grad_d_mod,
        grad_d_att,
        grad_d_merge,
        grad_d_gate,
        grad_d_lift,
        grad_d_lower,
        grad_time,
        gain_total[1],
    )


def solution(mesh):
    return jax.shard_map(
        functools.partial(per_device, mesh.shape["dp"], mesh.shape["noise"]),
        mesh=mesh,
        in_specs=(
            P(("dp", "noise"), None, None),
            P("noise", "dp", None, None),
            P("noise", "dp"),
            P(("dp", "noise")),
            P("noise", "dp", None, None),
            P("dp", "noise"),
            P("dp", "noise"),
            P("dp", "noise"),
            P("dp", "noise"),
            P("dp", "noise"),
            P("dp", "noise"),
            P("dp", "noise"),
            P(),
            P("dp", "noise"),
            P("dp", "noise"),
            P("dp", "noise"),
            P("dp", "noise"),
            P("dp", "noise"),
            P("dp", "noise"),
            P("dp", "noise"),
            P(),
        ),
        out_specs=(
            P("noise", "dp", None, None),
            P(("dp", "noise"), None, None),
            P(("dp", "noise"), None, None),
            P("dp", "noise"),
            P("dp", "noise"),
            P("dp", "noise"),
            P("dp", "noise"),
            P("dp", "noise"),
            P("dp", "noise"),
            P("dp", "noise"),
            P(),
            P("dp", "noise"),
            P("dp", "noise"),
            P("dp", "noise"),
            P("dp", "noise"),
            P("dp", "noise"),
            P("dp", "noise"),
            P("dp", "noise"),
            P(),
        ),
        check_vma=False,
    )
```

```python
import functools
import math

import jax
import jax.numpy as jnp
import numpy as np
from jax import lax
from jax.experimental import pallas as pl
from jax.experimental.pallas import tpu as pltpu
from jax.sharding import PartitionSpec as P

HEADS = 16
HEAD = 72
NT = 1000
GRID = 8


EPS = 1e-06


def angle_tables(length):
    places = np.arange(length)
    quarter = HEAD // 4
    freqs = np.exp(-math.log(10000.0) * np.arange(quarter) / quarter)
    row_angle = (places // GRID)[:, None] * freqs[None, :]
    col_angle = (places % GRID)[:, None] * freqs[None, :]
    return (row_angle, col_angle)


def sinusoid(times, width):
    half = width // 2
    freqs = jnp.exp(-math.log(10000.0) * jnp.arange(half).astype(jnp.float32) / half)
    angle = (times * 1000.0)[..., None] * freqs
    return jnp.concatenate([jnp.cos(angle), jnp.sin(angle)], -1)


BF = jnp.bfloat16
F32 = jnp.float32


def dot(left, right):
    return jnp.dot(left, right, preferred_element_type=F32)


def dot_nt(left, right):
    return lax.dot_general(left, right, (((1,), (1,)), ((), ())), preferred_element_type=F32)


def dot_tn(left, right):
    return lax.dot_general(left, right, (((0,), (0,)), ((), ())), preferred_element_type=F32)


def dot_tt(left, right):
    return lax.dot_general(left, right, (((0,), (1,)), ((), ())), preferred_element_type=F32)


def pick(array, index, axis=0):
    return lax.dynamic_index_in_dim(array, index, axis, keepdims=False)


class Noise:
    def __init__(self, count):
        self.count = count
        self.me = lax.axis_index("noise")
        self.quick = count == 4

    def swap(self, array, mask):
        return lax.ppermute(array, "noise", [(n, n ^ mask) for n in range(self.count)])

    def order(self, near):
        odd = self.me % 2 == 1
        far = self.me // 2 == 1
        near = [
            jnp.where(odd, near[1], near[0]),
            jnp.where(odd, near[0], near[1]),
            jnp.where(odd, near[3], near[2]),
            jnp.where(odd, near[2], near[3]),
        ]
        return [
            jnp.where(far, near[2], near[0]),
            jnp.where(far, near[3], near[1]),
            jnp.where(far, near[0], near[2]),
            jnp.where(far, near[1], near[3]),
        ]

    def gather(self, array):
        if not self.quick:
            whole = lax.all_gather(array, "noise", axis=0, tiled=False)
            return [whole[n] for n in range(self.count)]
        across = self.swap(array, 2)
        beside = self.swap(array, 1)
        corner = self.swap(across, 1)
        return self.order([array, beside, across, corner])

    def near(self, array):
        across = self.swap(array, 2)
        beside = self.swap(array, 1)
        return [array, beside, across, self.swap(across, 1)]

    def near_sum(self, keep, send):
        half = keep.astype(F32) + self.swap(send, 1).astype(F32)
        return half[0] + self.swap(half[1].astype(BF), 2).astype(F32)

    def scatter_sum(self, blocks, wire=BF):
        if not self.quick:
            return lax.psum_scatter(
                blocks.astype(wire), "noise", scatter_dimension=0, tiled=False
            ).astype(F32)
        core = self.me % 2
        far = self.me // 2
        pairs = blocks.reshape((2, 2) + blocks.shape[1:])
        keep = pick(pairs, core, 1).astype(F32)
        send = pick(pairs, 1 - core, 1).astype(wire)
        half = keep + self.swap(send, 1).astype(F32)
        return pick(half, far) + self.swap(pick(half, 1 - far).astype(wire), 2).astype(F32)

    def total(self, array):
        if not self.quick:
            return lax.psum(array, "noise")
        array = array + self.swap(array, 1)
        return array + self.swap(array, 2)

    def exchange(self, blocks):
        if not self.quick:
            whole = lax.all_to_all(blocks, "noise", 0, 0)
            return [whole[n] for n in range(self.count)]
        near = [pick(blocks, self.me)]
        for mask in (1, 2, 3):
            near.append(self.swap(pick(blocks, self.me ^ mask), mask))
        return self.order(near)


class Groups:
    def __init__(self, count):
        self.count = count
        self.quick = count == 8
        self.sides = 2
        self.line = count // 2
        self.place = lax.axis_index("dp")
        self.spot = self.place // self.sides
        self.side = self.place % self.sides
        self.across = [
            (z * 2 + x, z * 2 + 1 - x) for z in range(self.line) for x in range(2)
        ]

    def shift(self, array, spots, step):
        pairs = [(z * 2 + x, (z + step) * 2 + x) for z in spots for x in range(2)]
        return lax.ppermute(array, "dp", pairs)

    def turn(self, array, step):
        pairs = [
            (z * 2 + x, (z + step) % self.line * 2 + x)
            for z in range(self.line)
            for x in range(2)
        ]
        return lax.ppermute(array, "dp", pairs)

    def swap(self, array, mask):
        return lax.ppermute(array, "dp", [(n, n ^ mask) for n in range(self.count)])

    def gather_whole(self, array):
        return lax.all_gather(array, "dp", axis=0, tiled=False)

    def sum_whole(self, blocks):
        return lax.psum_scatter(
            blocks.astype(BF), "dp", scatter_dimension=0, tiled=False
        ).astype(F32)

    def gather(self, array):
        if not self.quick:
            return self.gather_whole(array), array
        near = [array] + [self.turn(array, step) for step in (1, 2, 3)]
        far = [lax.ppermute(part, "dp", self.across) for part in near]
        return place_blocks(self.place.reshape(1), near + far), near[3]

    def scatter_sum(self, blocks, wire=BF):
        if not self.quick:
            return self.sum_whole(blocks)
        pairs = blocks.reshape((self.line, 2) + blocks.shape[1:])
        keep = pick(pairs, self.side, 1).astype(F32)
        send = pick(pairs, 1 - self.side, 1).astype(wire)
        half = keep + lax.ppermute(send, "dp", self.across).astype(F32)
        total = pick(half, self.spot)
        for step in (1, 3, 2):
            part = pick(half, (self.spot + step) % self.line).astype(wire)
            total = total + self.turn(part, step).astype(F32)
        return total

    def gather_small(self, array):
        if not self.quick:
            return self.gather_whole(array)
        array = array[None]
        for mask in (1, 2, 4):
            other = self.swap(array, mask)
            high = (self.place // mask) % 2 == 1
            array = jnp.where(
                high, jnp.concatenate([other, array]), jnp.concatenate([array, other])
            )
        return array

    def gather_direct(self, array):
        if not self.quick:
            return self.gather_whole(array)
        came = [array]
        for step in range(1, self.count):
            pairs = [(n, (n + step) % self.count) for n in range(self.count)]
            came.append(lax.ppermute(array, "dp", pairs))
        turned = jnp.stack((came + came)[::-1])
        return lax.dynamic_slice_in_dim(turned, self.count - 1 - self.place, self.count, 0)

    def sum_small(self, blocks):
        if not self.quick:
            return lax.psum_scatter(blocks, "dp", scatter_dimension=0, tiled=False)
        for mask in (4, 2, 1):
            halves = blocks.reshape((2, -1) + blocks.shape[1:])
            high = (self.place // mask) % 2
            blocks = pick(halves, high) + self.swap(pick(halves, 1 - high), mask)
        return blocks[0]

    def total(self, array):
        if not self.quick:
            return lax.psum(array, "dp")
        for mask in (1, 2, 4):
            array = array + self.swap(array, mask)
        return array


def split_pieces(noise, weight, pieces):
    count = noise.count
    rows, width = weight.shape
    chunk = width // pieces
    slots = -(-pieces // count)
    parts = jnp.moveaxis(weight.reshape(rows, pieces, chunk), 1, 0)
    parts = jnp.concatenate(
        [parts, jnp.zeros((slots * count - pieces, rows, chunk), weight.dtype)]
    ).reshape(slots, count, rows, chunk)
    parts = jnp.roll(parts, pieces * noise.me, axis=1)
    return jnp.moveaxis(parts, 1, 0)


def take_pieces(noise, came, pieces):
    count = noise.count
    out = []
    for piece in range(pieces):
        chunk = count * piece + noise.me
        out.append(came[chunk // pieces, (chunk % pieces) // count])
    return jnp.stack(out, 1)


def return_pieces(noise, grad):
    count = noise.count
    pieces = grad.shape[1]
    slots = -(-pieces // count)
    rows = []
    for target in range(count):
        first = (noise.me - pieces * target) % count
        line = []
        for slot in range(slots):
            turn = jnp.minimum(first + slot * count, pieces - 1)
            line.append(pick(grad, (pieces * target + turn) // count, 1))
        rows.append(jnp.stack(line))
    return jnp.stack(rows)


def join_pieces(noise, came, pieces):
    count = noise.count
    out = []
    for turn in range(pieces):
        chunk = pieces * noise.me + turn
        out.append(came[chunk % count, turn // count])
    joined = jnp.stack(out, 1)
    return joined.reshape(joined.shape[0], -1)


def split_units(noise, groups, weight):
    count = noise.count
    rows, width = weight.shape
    low = groups.count // count
    parts = weight.reshape(rows, low, count, width // (low * count))
    return parts.transpose(2, 0, 1, 3).reshape(count, rows, width // count)


def take_units(noise, groups, came):
    count, rows, width = came.shape
    return jnp.moveaxis(came, 0, 1).reshape(rows, count * width)


def return_units(noise, grad):
    rows, width = grad.shape
    return jnp.moveaxis(grad.reshape(rows, noise.count, width // noise.count), 1, 0)


def join_units(noise, groups, came):
    count, rows, width = came.shape
    low = groups.count // count
    parts = came.reshape(count, rows, low, width // low)
    return parts.transpose(1, 2, 0, 3).reshape(rows, count * width)


def place_weights(noise, groups, w_att, w_gate, w_lift, w_lower, w_mod=None):
    rows = w_att.shape[0]
    att = split_pieces(noise, w_att, 3)
    chunk = att.shape[-1]
    parts = [att.reshape(noise.count, rows, chunk)]
    if w_mod is not None:
        mod = split_pieces(noise, w_mod, 6)
        parts += [mod[:, 0], mod[:, 1]]
    parts.append(split_units(noise, groups, w_gate))
    parts.append(split_units(noise, groups, w_lift))
    unit = parts[-1].shape[-1]
    parts.append(w_lower.reshape(noise.count, rows, unit))
    came = jnp.stack(noise.exchange(jnp.concatenate(parts, -1)))
    spot = 0
    out = [take_pieces(noise, came[:, None, :, :chunk], 3)]
    spot = chunk
    if w_mod is not None:
        mod = jnp.stack([came[:, :, chunk : 2 * chunk], came[:, :, 2 * chunk : 3 * chunk]], 1)
        out.append(take_pieces(noise, mod, 6))
        spot = 3 * chunk
    out.append(take_units(noise, groups, came[:, :, spot : spot + unit]))
    spot += unit
    out.append(take_units(noise, groups, came[:, :, spot : spot + unit]))
    spot += unit
    lower = came[:, :, spot:].reshape(noise.count, -1, w_lower.shape[1])
    lower = jnp.moveaxis(lower, 0, 1)
    out.append(lower.reshape(lower.shape[0], -1))
    return out


def flat(weight):
    return weight.reshape(weight.shape[0] * weight.shape[1], -1)


def norm_parts(value):
    mean = jnp.mean(value, -1, keepdims=True)
    center = value - mean
    inverse = lax.rsqrt(jnp.mean(center * center, -1, keepdims=True) + EPS)
    return center * inverse, inverse


def norm_back(grad, normed, inverse):
    first = jnp.mean(grad, -1, keepdims=True)
    second = jnp.mean(grad * normed, -1, keepdims=True)
    return inverse * (grad - first - normed * second)


def silu_slope(value):
    gate = jax.nn.sigmoid(value)
    return gate * (1.0 + value * (1.0 - gate))


VMEM_BYTES = 48 * 1024 * 1024
STEP = 256


def kernel_call(kernel, grid, ins, outs, scratch=(), scalars=1):
    return pl.pallas_call(
        kernel,
        out_shape=[shape for shape, _ in outs],
        grid_spec=pltpu.PrefetchScalarGridSpec(
            num_scalar_prefetch=scalars,
            grid=grid,
            in_specs=ins,
            out_specs=[spec for _, spec in outs],
            scratch_shapes=list(scratch),
        ),
        compiler_params=pltpu.CompilerParams(vmem_limit_bytes=VMEM_BYTES),
    )


def row_spec(width):
    return pl.BlockSpec((STEP, width), lambda n, *_: (n, 0))


def up_spec(width):
    return pl.BlockSpec((width, STEP), lambda n, *_: (0, n))


def full_spec(shape):
    return pl.BlockSpec(shape, lambda n, *_: (0,) * len(shape))


def shaped(shape, dtype):
    return jax.ShapeDtypeStruct(shape, dtype)


def joined(me_ref, near, parts):
    for n, ref in enumerate(near):
        parts[me_ref[0] ^ n] = ref[...]
    return jnp.concatenate([parts[n] for n in range(4)])


def near_scratch(near):
    return [pltpu.VMEM((4, near[0].shape[0], STEP), BF)]


def place_kernel(place_ref, *refs):
    blocks, out_ref, sems = refs[:8], refs[8], refs[9]
    spot, side = place_ref[0] // 2, place_ref[0] % 2
    copies = []
    for n, ref in enumerate(blocks):
        line = (spot + 4 - n % 4) % 4
        at = line * 2 + (side if n < 4 else 1 - side)
        copies.append(pltpu.make_async_copy(ref, out_ref.at[at], sems.at[n]))
    for copy in copies:
        copy.start()
    for copy in copies:
        copy.wait()


def place_blocks(place, blocks):
    block = blocks[0]
    return pl.pallas_call(
        place_kernel,
        out_shape=shaped((len(blocks),) + block.shape, block.dtype),
        in_specs=[pl.BlockSpec(memory_space=pltpu.SMEM)]
        + [pl.BlockSpec(memory_space=pl.ANY)] * len(blocks),
        out_specs=pl.BlockSpec(memory_space=pl.ANY),
        scratch_shapes=[pltpu.SemaphoreType.DMA((len(blocks),))],
        compiler_params=pltpu.CompilerParams(vmem_limit_bytes=8 * 1024 * 1024),
    )(place, *blocks)


def join_kernel(upward, me_ref, x0, x1, x2, x3, w_ref, full_ref, out_ref, parts):
    whole = joined(me_ref, (x0, x1, x2, x3), parts)
    full_ref[...] = whole
    if upward:
        out_ref[...] = dot_tn(w_ref[...], whole)
    else:
        out_ref[...] = dot_tn(whole, w_ref[...])


def join_dot(me, near, weight, upward=False):
    quarter, rows = near[0].shape
    width = weight.shape[1]
    if upward:
        out = (shaped((width, rows), F32), up_spec(width))
    else:
        out = (shaped((rows, width), F32), row_spec(width))
    return kernel_call(
        functools.partial(join_kernel, upward),
        (rows // STEP,),
        [up_spec(quarter)] * 4 + [full_spec(weight.shape)],
        [(shaped((4 * quarter, rows), BF), up_spec(4 * quarter)), out],
        near_scratch(near),
    )(me, *near, weight)


def units_kernel(me_ref, x0, x1, x2, x3, w_ref, full_ref, out_ref, hid_ref, parts):
    whole = joined(me_ref, (x0, x1, x2, x3), parts)
    full_ref[...] = whole
    acts = dot_tn(whole, w_ref[...])
    out_ref[...] = acts
    unit = hid_ref.shape[1]
    hid_ref[...] = (jax.nn.silu(acts[:, :unit]) * acts[:, unit:]).astype(BF)


def units_dot(me, near, weight):
    quarter, rows = near[0].shape
    width = weight.shape[1]
    return kernel_call(
        units_kernel,
        (rows // STEP,),
        [up_spec(quarter)] * 4 + [full_spec(weight.shape)],
        [
            (shaped((4 * quarter, rows), BF), up_spec(4 * quarter)),
            (shaped((rows, width), F32), row_spec(width)),
            (shaped((rows, width // 2), BF), row_spec(width // 2)),
        ],
        near_scratch(near),
    )(me, *near, weight)


def lower_kernel(me_ref, x0, x1, x2, x3, w_ref, full_ref, out_ref, parts):
    whole = joined(me_ref, (x0, x1, x2, x3), parts).T
    full_ref[...] = whole
    out_ref[...] = dot_nt(whole, w_ref[...])


def lower_back_dot(me, near, weight):
    quarter, rows = near[0].shape
    width = weight.shape[0]
    return kernel_call(
        lower_kernel,
        (rows // STEP,),
        [up_spec(quarter)] * 4 + [full_spec(weight.shape)],
        [
            (shaped((rows, 4 * quarter), BF), row_spec(4 * quarter)),
            (shaped((rows, width), F32), row_spec(width)),
        ],
        near_scratch(near),
    )(me, *near, weight)


def give(parts, keep_ref, send_ref):
    keep_ref[0] = parts[0]
    keep_ref[1] = parts[2]
    send_ref[0] = parts[1]
    send_ref[1] = parts[3]


def give_outs(rows, quarter):
    pair = pl.BlockSpec((2, quarter, STEP), lambda n, *_: (0, 0, n))
    return [(shaped((2, quarter, rows), BF), pair)] * 2


def spread_kernel(me_ref, y_ref, w_ref, keep_ref, send_ref, parts):
    quarter = keep_ref.shape[1]
    value = y_ref[...]
    for n in range(4):
        term = dot_nt(w_ref[n * quarter : (n + 1) * quarter], value)
        parts[me_ref[0] ^ n] = term.astype(BF)
    give(parts, keep_ref, send_ref)


def spread_dot(me, value, weight):
    rows, width = value.shape
    quarter = weight.shape[0] // 4
    return kernel_call(
        spread_kernel,
        (rows // STEP,),
        [row_spec(width), full_spec(weight.shape)],
        give_outs(rows, quarter),
        [pltpu.VMEM((4, quarter, STEP), BF)],
    )(me, value, weight)


def spread_up_kernel(me_ref, y_ref, w_ref, keep_ref, send_ref, parts):
    quarter = keep_ref.shape[1]
    value = y_ref[...]
    for n in range(4):
        term = dot(w_ref[n * quarter : (n + 1) * quarter], value)
        parts[me_ref[0] ^ n] = term.astype(BF)
    give(parts, keep_ref, send_ref)


def spread_up_dot(me, value, weight):
    width, rows = value.shape
    quarter = weight.shape[0] // 4
    return kernel_call(
        spread_up_kernel,
        (rows // STEP,),
        [up_spec(width), full_spec(weight.shape)],
        give_outs(rows, quarter),
        [pltpu.VMEM((4, quarter, STEP), BF)],
    )(me, value, weight)


def lowered_kernel(me_ref, y_ref, w_ref, keep_ref, send_ref, parts):
    quarter = keep_ref.shape[1]
    term = dot(y_ref[...], w_ref[...]).astype(BF).T
    for n in range(4):
        parts[me_ref[0] ^ n] = term[n * quarter : (n + 1) * quarter]
    give(parts, keep_ref, send_ref)


def lowered_dot(me, value, weight):
    rows, width = value.shape
    quarter = weight.shape[1] // 4
    return kernel_call(
        lowered_kernel,
        (rows // STEP,),
        [row_spec(width), full_spec(weight.shape)],
        give_outs(rows, quarter),
        [pltpu.VMEM((4, quarter, STEP), BF)],
    )(me, value, weight)


def acts_back_kernel(me_ref, g_ref, a_ref, w_ref, acts_ref, keep_ref, send_ref, parts):
    quarter = keep_ref.shape[1]
    unit = g_ref.shape[1]
    grad = g_ref[...]
    gate_act, lift_act = a_ref[:, :unit], a_ref[:, unit:]
    gate = jax.nn.sigmoid(gate_act)
    slope = gate * (1.0 + gate_act * (1.0 - gate))
    acts_ref[:, :unit] = (grad * lift_act * slope).astype(BF)
    acts_ref[:, unit:] = (grad * (gate_act * gate)).astype(BF)
    value = acts_ref[...]
    for n in range(4):
        term = dot_nt(w_ref[n * quarter : (n + 1) * quarter], value)
        parts[me_ref[0] ^ n] = term.astype(BF)
    give(parts, keep_ref, send_ref)


def acts_back(me, grad, acts, weight):
    rows, unit = grad.shape
    quarter = weight.shape[0] // 4
    return kernel_call(
        acts_back_kernel,
        (rows // STEP,),
        [row_spec(unit), row_spec(2 * unit), full_spec(weight.shape)],
        [(shaped((rows, 2 * unit), BF), row_spec(2 * unit))] + give_outs(rows, quarter),
        [pltpu.VMEM((4, quarter, STEP), BF)],
    )(me, grad, acts, weight)


def grad_kernel(x_ref, y_ref, out_ref):
    out_ref[...] = dot(x_ref[...], y_ref[...]).astype(BF)


def grad_turned_kernel(x_ref, y_ref, out_ref):
    out_ref[...] = dot_nt(x_ref[...], y_ref[...]).astype(BF)


def grad_low_kernel(x_ref, y_ref, out_ref):
    out_ref[...] = dot_tn(x_ref[...], y_ref[...]).astype(BF)


def grad_dot(left, right, kernel=grad_kernel):
    step = 384
    low = kernel is grad_low_kernel
    width, rows = left.shape[::-1] if low else left.shape
    wide = right.shape[0] if kernel is grad_turned_kernel else right.shape[1]
    if low:
        spec = pl.BlockSpec((rows, step), lambda n: (0, n))
    else:
        spec = pl.BlockSpec((step, rows), lambda n: (n, 0))
    return pl.pallas_call(
        kernel,
        out_shape=shaped((width, wide), BF),
        grid=(width // step,),
        in_specs=[spec, pl.BlockSpec(right.shape, lambda n: (0, 0))],
        out_specs=pl.BlockSpec((step, wide), lambda n: (n, 0)),
        compiler_params=pltpu.CompilerParams(vmem_limit_bytes=VMEM_BYTES),
    )(left, right)


def mod_kernel(x_ref, w_ref, out_ref):
    out_ref[...] = dot(x_ref[...], w_ref[...]).T


def mod_dot(value, weight):
    rows, width = value.shape
    wide = weight.shape[1]
    return kernel_call(
        mod_kernel,
        (rows // STEP,),
        [row_spec(width), full_spec(weight.shape)],
        [(shaped((wide, rows), F32), up_spec(wide))],
        scalars=0,
    )(value, weight)[0]


def mod_back_kernel(*refs):
    parts, (w_ref, cat_ref, out_ref) = refs[:6], refs[6:]
    grad = jnp.concatenate([ref[...] for ref in parts]).T
    cat_ref[...] = grad
    out_ref[...] = dot_nt(grad, w_ref[...])


def mod_back(parts, weight):
    quarter, rows = parts[0].shape
    return kernel_call(
        mod_back_kernel,
        (rows // STEP,),
        [up_spec(quarter)] * 6 + [full_spec(weight.shape)],
        [
            (shaped((rows, 6 * quarter), BF), row_spec(6 * quarter)),
            (shaped((rows, weight.shape[0]), F32), row_spec(weight.shape[0])),
        ],
        scalars=0,
    )(*parts, weight)


def kind_width(kind, quarter):
    if kind[0] == "pieces":
        return -(-kind[1] // 4) * quarter
    if kind[0] == "units":
        return kind[1] // 4
    return quarter


def pack_parts(me, kinds, low, quarter):
    out = []
    spot = 0
    for item, kind in enumerate(kinds):
        for far in range(4):
            to = me ^ far
            if kind[0] == "pieces":
                count = kind[1]
                for slot in range(-(-count // 4)):
                    turn = (to - count * me) % 4 + 4 * slot
                    if turn < count:
                        out.append(
                            (item, far, None, turn * quarter, spot + slot * quarter, quarter)
                        )
            elif kind[0] == "units":
                each = kind[1] // (4 * low)
                for n in range(low):
                    at = n * 4 * each + to * each
                    out.append((item, far, None, at, spot + n * each, each))
            else:
                out.append((item, far, (to * kind[1], kind[1]), 0, spot, quarter))
        spot += kind_width(kind, quarter)
    return out


def unpack_parts(me, kinds, low, quarter):
    out = []
    spot = 0
    for item, kind in enumerate(kinds):
        for far in range(4):
            come = me ^ far
            if kind[0] == "pieces":
                count = kind[1]
                for slot in range(-(-count // 4)):
                    turn = (me - count * come) % 4 + 4 * slot
                    if turn < count:
                        piece = (count * come + turn) // 4
                        out.append(
                            (item, far, None, piece * quarter, spot + slot * quarter, quarter)
                        )
            elif kind[0] == "units":
                each = kind[1] // (4 * low)
                for n in range(low):
                    at = (come * low + n) * each
                    out.append((item, far, None, at, spot + n * each, each))
            else:
                out.append((item, far, (0, kind[1]), come * quarter, spot, quarter))
        spot += kind_width(kind, quarter)
    return out


def pack_kernel(plan, me_ref, *refs):
    items, out_ref = refs[:-1], refs[-1]
    out_ref[...] = jnp.zeros_like(out_ref)
    for me in range(4):

        @pl.when(me_ref[0] == me)
        def _():
            for item, far, lines, at, spot, size in plan(me):
                first, count = lines or (0, out_ref.shape[1])
                out_ref[far, :count, spot : spot + size] = items[item][
                    first : first + count, at : at + size
                ].astype(BF)


def unpack_kernel(plan, me_ref, *refs):
    packets, outs = refs[:4], refs[4:]
    for me in range(4):

        @pl.when(me_ref[0] == me)
        def _():
            for item, far, lines, at, spot, size in plan(me):
                first, count = lines or (0, packets[0].shape[0])
                outs[item][first : first + count, at : at + size] = packets[far][
                    :count, spot : spot + size
                ].astype(outs[item].dtype)


def whole_call(kernel, outs, me, args):
    return kernel_call(
        kernel,
        (1,),
        [full_spec(arg.shape) for arg in args],
        [(out, full_spec(out.shape)) for out in outs],
    )(me, *args)


def trade(noise, me, arrays, kinds, low, back, shapes, dtype):
    quarter = kind_quarter(kinds, arrays, back)
    width = sum(kind_width(kind, quarter) for kind in kinds)
    lines = max(a.shape[0] for a, kind in zip(arrays, kinds) if kind[0] != "lower")
    there, here = (unpack_parts, pack_parts) if back else (pack_parts, unpack_parts)
    packed = whole_call(
        functools.partial(
            pack_kernel, functools.partial(there, kinds=kinds, low=low, quarter=quarter)
        ),
        [shaped((4, lines, width), BF)],
        me,
        arrays,
    )[0]
    near = [packed[0]] + [noise.swap(packed[n], n) for n in (1, 2, 3)]
    return whole_call(
        functools.partial(
            unpack_kernel, functools.partial(here, kinds=kinds, low=low, quarter=quarter)
        ),
        [shaped(shape, dtype) for shape in shapes],
        me,
        near,
    )


def kind_quarter(kinds, arrays, back):
    for array, kind in zip(arrays, kinds):
        if kind[0] == "pieces":
            return array.shape[1] // kind[1]
        if kind[0] == "lower":
            return array.shape[1] // 4 if back else array.shape[1]


def attend_tables(length, repeat, gains):
    heads = HEADS // 4
    row_angle, col_angle = angle_tables(length)
    angle = np.concatenate([row_angle, row_angle, col_angle, col_angle], -1)
    angle = np.tile(angle, (repeat, heads))
    spread = jnp.tile(gains, (1, heads))
    return jnp.asarray(np.cos(angle), F32), jnp.asarray(np.sin(angle), F32), spread


def attend_matrices():
    width = HEADS // 4 * HEAD
    quarter = HEAD // 4
    index = np.arange(width)
    same = (index[:, None] // HEAD == index[None, :] // HEAD).astype(np.float32)
    second = (index % (2 * quarter)) >= quarter
    source = np.where(second, index - quarter, index + quarter)
    turn = np.zeros((width, width), np.float32)
    turn[source, index] = np.where(second, 1.0, -1.0)
    low = jnp.asarray(same, BF), jnp.asarray(turn, BF), jnp.asarray(turn.T, BF)
    return low


def low_dot(value, matrix):
    return dot(value.astype(BF), matrix)


def head_masks(width):
    lane = lax.broadcasted_iota(jnp.int32, (1, width), 1)
    return [
        jnp.logical_and(lane >= n * HEAD, lane < (n + 1) * HEAD).astype(F32)
        for n in range(width // HEAD)
    ]


def ready_heads(value, gain, cosine, sine, same, turn):
    inverse = lax.rsqrt(low_dot(value * value, same) * (1.0 / HEAD) + EPS)
    normed = value * inverse
    scaled = normed * gain
    turned = scaled * cosine + low_dot(scaled, turn) * sine
    return turned.astype(BF), normed, inverse


def stack_heads(value, masks):
    value = value.astype(F32)
    return jnp.concatenate([value * mask for mask in masks]).astype(BF)


def fold_heads(value, masks, length):
    out = value[:length] * masks[0]
    for n in range(1, len(masks)):
        out = out + value[n * length : (n + 1) * length] * masks[n]
    return out


def prob_of(stacked, keys_low):
    scores = dot_nt(stacked, keys_low) * HEAD ** (-0.5)
    grown = jnp.exp(scores - jnp.max(scores, -1, keepdims=True))
    return grown / jnp.sum(grown, -1, keepdims=True)


def attend_kernel(
    length,
    upward,
    p_ref,
    cos_ref,
    sin_ref,
    gain_ref,
    same_ref,
    turn_ref,
    out_ref,
    mixed_ref,
):
    width = mixed_ref.shape[1]
    q_ref, k_ref, v_ref = [p_ref[:, n * width : (n + 1) * width] for n in range(3)]
    masks = head_masks(width)
    same, turn = same_ref[...], turn_ref[...]
    cosine, sine = cos_ref[...], sin_ref[...]
    query, _, _ = ready_heads(q_ref, gain_ref[0:1], cosine, sine, same, turn)
    key, _, _ = ready_heads(k_ref, gain_ref[1:2], cosine, sine, same, turn)
    value = v_ref.astype(BF)
    for image in range(mixed_ref.shape[0] // length):
        part = slice(image * length, (image + 1) * length)
        prob = prob_of(stack_heads(query[part], masks), key[part])
        mixed = dot(prob.astype(BF), value[part])
        mixed_ref[part] = fold_heads(mixed, masks, length)
    if upward:
        out_ref[...] = mixed_ref[...].T.astype(BF)
    else:
        out_ref[...] = mixed_ref[...].astype(BF)


def attend_back_kernel(
    length,
    upward,
    p_ref,
    cos_ref,
    sin_ref,
    gain_ref,
    same_ref,
    turn_ref,
    back_ref,
    grad_ref,
    dp_ref,
    dg_ref,
    gq_ref,
    gk_ref,
    gv_ref,
):
    width = gq_ref.shape[1]
    q_ref, k_ref, v_ref = [p_ref[:, n * width : (n + 1) * width] for n in range(3)]
    masks = head_masks(width)
    same, turn, back = same_ref[...], turn_ref[...], back_ref[...]
    cosine, sine = cos_ref[...], sin_ref[...]
    query, q_norm, q_inv = ready_heads(q_ref, gain_ref[0:1], cosine, sine, same, turn)
    key, k_norm, k_inv = ready_heads(k_ref, gain_ref[1:2], cosine, sine, same, turn)
    value = v_ref.astype(BF)
    grad = grad_ref[...].T if upward else grad_ref[...]
    for image in range(q_ref.shape[0] // length):
        part = slice(image * length, (image + 1) * length)
        stacked = stack_heads(query[part], masks)
        prob = prob_of(stacked, key[part])
        grads = stack_heads(grad[part], masks)
        gv_ref[part] = dot_tn(prob.astype(BF), grads)
        g_prob = dot_nt(grads, value[part])
        g_score = prob * (g_prob - jnp.sum(g_prob * prob, -1, keepdims=True))
        g_score = g_score.astype(BF)
        gq_ref[part] = fold_heads(dot(g_score, key[part]), masks, length)
        gk_ref[part] = dot_tn(g_score, stacked)

    @pl.when(pl.program_id(0) == 0)
    def _():
        dg_ref[...] = jnp.zeros_like(dg_ref)

    for n, (g_ref, normed, inverse) in enumerate(
        ((gq_ref, q_norm, q_inv), (gk_ref, k_norm, k_inv))
    ):
        turned = g_ref[...] * HEAD ** (-0.5)
        scaled = turned * cosine + low_dot(turned * sine, back)
        dg_ref[n : n + 1] += jnp.sum(scaled * normed, 0, keepdims=True)
        weighed = scaled * gain_ref[n : n + 1]
        mean = low_dot(weighed * normed, same) * (1.0 / HEAD)
        out = inverse * (weighed - normed * mean)
        dp_ref[:, n * width : (n + 1) * width] = out.astype(BF)
    dp_ref[:, 2 * width :] = gv_ref[...].astype(BF)


def attend_blocks(rows, length, width):
    step = STEP

    def row(size):
        return pl.BlockSpec((step, size), lambda n: (n, 0))

    def whole(*shape):
        return pl.BlockSpec(shape, lambda n: (0, 0))

    return step, row, whole


def attend_forward(project, gains, length, upward=False):
    rows, width = project.shape[0], project.shape[1] // 3
    step, row, whole = attend_blocks(rows, length, width)
    cosine, sine, spread = attend_tables(length, step // length, gains)
    same, turn, _ = attend_matrices()
    return pl.pallas_call(
        functools.partial(attend_kernel, length, upward),
        out_shape=shaped((width, rows) if upward else (rows, width), BF),
        grid=(rows // step,),
        in_specs=[row(3 * width), whole(step, width), whole(step, width), whole(2, width)]
        + [whole(width, width)] * 2,
        out_specs=up_spec(width) if upward else row(width),
        scratch_shapes=[pltpu.VMEM((step, width), F32)],
        compiler_params=pltpu.CompilerParams(vmem_limit_bytes=VMEM_BYTES),
    )(project, cosine, sine, spread, same, turn)


def attend_backward(grad_low, gains, project, length, upward=False):
    rows, width = project.shape[0], project.shape[1] // 3
    step, row, whole = attend_blocks(rows, length, width)
    cosine, sine, spread = attend_tables(length, step // length, gains)
    same, turn, back = attend_matrices()
    grad, gain_grad = pl.pallas_call(
        functools.partial(attend_back_kernel, length, upward),
        out_shape=(shaped((rows, 3 * width), BF), shaped((2, width), F32)),
        grid=(rows // step,),
        in_specs=[row(3 * width), whole(step, width), whole(step, width), whole(2, width)]
        + [whole(width, width)] * 3
        + [up_spec(width) if upward else row(width)],
        out_specs=(row(3 * width), whole(2, width)),
        scratch_shapes=[pltpu.VMEM((step, width), F32)] * 3,
        compiler_params=pltpu.CompilerParams(vmem_limit_bytes=VMEM_BYTES),
    )(project, cosine, sine, spread, same, turn, back, grad_low)
    return grad, jnp.sum(gain_grad.reshape(2, width // HEAD, HEAD), 1)


def per_device(
    groups_count,
    noise_count,
    clean_tokens,
    noise_tokens,
    time_index,
    class_label,
    velocity_cotangent,
    encoder_modulate,
    encoder_attend,
    encoder_merge,
    encoder_gate,
    encoder_lift,
    encoder_lower,
    class_table,
    encoder_gains,
    decoder_modulate,
    decoder_attend,
    decoder_merge,
    decoder_gate,
    decoder_lift,
    decoder_lower,
    time_weight,
    decoder_gains,
):
    noise = Noise(noise_count)
    groups = Groups(groups_count)
    own_images, length, width = clean_tokens.shape
    images = own_images * noise_count
    levels = noise_count
    quarter = width // noise_count
    own_rows = own_images * length
    rows = images * length
    place = noise.me * quarter

    def columns(value):
        return lax.dynamic_slice_in_dim(value, place, quarter, value.ndim - 1)

    def column_blocks(value):
        return jnp.moveaxis(value.reshape(value.shape[0], noise_count, quarter), 1, 0)

    def token_blocks(value):
        return value.reshape(noise_count, own_rows, width)

    facts = jnp.concatenate([class_label, time_index[0]])
    facts = jnp.stack(noise.gather(facts))
    times = (facts[:, own_images:].astype(F32) + 0.5) / NT
    labels = groups.gather_small(facts[:, :own_images].reshape(-1)).reshape(-1)

    me = noise.me.reshape(1)
    unit = encoder_gate.shape[1]
    chunk_rows = encoder_attend.shape[0]
    lower_rows = encoder_lower.shape[0] // noise_count
    low_units = groups_count // noise_count
    e_kinds = (("pieces", 3), ("units", unit), ("units", unit), ("lower", lower_rows))
    d_kinds = e_kinds + (("pieces", 6),)
    shapes = ((chunk_rows, 3 * quarter), (chunk_rows, unit), (chunk_rows, unit))
    shapes += ((lower_rows, width), (chunk_rows, 6 * quarter))
    if groups.quick:
        e_att_s, e_gate_s, e_lift_s, e_lower_s = trade(
            noise,
            me,
            (encoder_attend, encoder_gate, encoder_lift, encoder_lower),
            e_kinds,
            low_units,
            False,
            shapes[:4],
            BF,
        )
    else:
        e_att_s, e_gate_s, e_lift_s, e_lower_s = place_weights(
            noise, groups, encoder_attend, encoder_gate, encoder_lift, encoder_lower
        )
    (
        e_att_s,
        e_gate_s,
        e_lift_s,
        e_lower_s,
        clean_tokens,
        noise_tokens,
        velocity_cotangent,
        decoder_attend,
        decoder_gate,
    ) = lax.optimization_barrier(
        (
            e_att_s,
            e_gate_s,
            e_lift_s,
            e_lower_s,
            clean_tokens,
            noise_tokens,
            velocity_cotangent,
            decoder_attend,
            decoder_gate,
        )
    )
    e_first, early = groups.gather(
        jnp.concatenate([e_att_s.reshape(chunk_rows, -1), encoder_merge], -1)
    )
    labels, early = lax.optimization_barrier((labels, early))

    here = class_table.shape[1]
    onehot = (
        labels[:, None] == (jnp.arange(here) + noise.me * here)[None, :]
    ).astype(BF)
    class_cond = noise.total(dot_nt(onehot, class_table))
    class_low = jax.nn.silu(class_cond).astype(BF)
    class_mod = dot(class_low, encoder_modulate)
    class_mod = groups.sum_small(
        class_mod.reshape(groups_count, images, class_mod.shape[1])
    )
    class_mod = jnp.concatenate(noise.gather(class_mod), -1)

    e_att = flat(e_first[:, :, : 3 * quarter])
    e_merge = flat(e_first[:, :, 3 * quarter :])
    e_second_s, _, _ = lax.optimization_barrier(
        (jnp.concatenate([e_gate_s, e_lift_s], -1), early, class_low)
    )
    e_pair, later = groups.gather(e_second_s)
    e_units = flat(e_pair)
    e_lower_s, _, class_mod = lax.optimization_barrier((e_lower_s, later, class_mod))
    e_lower = flat(groups.gather(e_lower_s)[0])
    if groups.quick:
        d_att_s, d_gate_s, d_lift_s, d_lower_s, d_mod_s = trade(
            noise,
            me,
            (decoder_attend, decoder_gate, decoder_lift, decoder_lower, decoder_modulate),
            d_kinds,
            low_units,
            False,
            shapes,
            BF,
        )
    else:
        d_att_s, d_mod_s, d_gate_s, d_lift_s, d_lower_s = place_weights(
            noise,
            groups,
            decoder_attend,
            decoder_gate,
            decoder_lift,
            decoder_lower,
            decoder_modulate,
        )
    d_first_s = jnp.concatenate(
        [
            d_mod_s.reshape(chunk_rows, -1),
            d_att_s.reshape(chunk_rows, -1),
            decoder_merge,
            time_weight,
        ],
        -1,
    )

    def pad_lower(part):
        ends = ((0, 0),) * (part.ndim - 1) + ((0, 2 * unit - width),)
        return jnp.pad(part, ends)

    d_second_s = jnp.concatenate(
        [jnp.concatenate([d_gate_s, d_lift_s], -1), pad_lower(d_lower_s)]
    )
    d_first_s, _, _, _ = lax.optimization_barrier((d_first_s, e_first, e_units, e_lower))
    d_whole = flat(groups.gather_whole(d_first_s))
    d_mod, d_att, d_merge, d_time = [
        d_whole[:, first * quarter : last * quarter]
        for first, last in ((0, 6), (6, 9), (9, 10), (10, 11))
    ]
    clean_group = jnp.concatenate(noise.gather(clean_tokens.reshape(own_rows, width)))
    clean_all = clean_group.astype(F32)
    own_times = (time_index[0].astype(F32) + 0.5) / NT
    own_ratio = jnp.repeat(own_times, length)[:, None]
    own_noise = noise_tokens[0].reshape(rows, width)
    own_cot = velocity_cotangent[0].reshape(rows, width)
    own_noisy = (1.0 - own_ratio) * clean_all + own_ratio * own_noise.astype(F32)
    own_mean = jnp.mean(own_noisy, -1)
    own_center = own_noisy - own_mean[:, None]
    own_inverse = lax.rsqrt(jnp.mean(own_center * own_center, -1) + EPS)
    stats = jnp.stack(noise.gather(jnp.stack([own_mean, own_inverse])))
    mean_one = stats[:, 0].reshape(1, -1)
    inverse_one = stats[:, 1].reshape(1, -1)
    came = noise.exchange(
        jnp.stack(
            [
                own_noise.T.reshape(noise_count, quarter, rows),
                own_cot.T.reshape(noise_count, quarter, rows),
            ],
            1,
        )
    )
    noise_cols = jnp.concatenate([part[0] for part in came], -1)
    cot_cols = jnp.concatenate([part[1] for part in came], -1).astype(F32)

    e_piece = [
        jnp.repeat(part, length, axis=0) for part in jnp.split(class_mod, 6, axis=-1)
    ]
    e_norm_one, e_inverse_one = norm_parts(clean_all)
    e_one = (e_norm_one * (1.0 + e_piece[1]) + e_piece[0]).astype(BF)
    e_heads = dot(e_one, e_att)
    e_mixed = attend_forward(e_heads, encoder_gains, length)
    e_mixed, d_second_s = lax.optimization_barrier((e_mixed, d_second_s))
    d_pair = groups.gather_whole(d_second_s)
    d_units = flat(d_pair[:, :chunk_rows])
    d_lower = flat(d_pair[:, chunk_rows:, :width])
    e_mixed_all = jnp.concatenate(noise.gather(e_mixed), -1)
    e_merged = jnp.concatenate(
        noise.gather(dot(e_mixed_all, e_merge).astype(BF)), -1
    ).astype(F32)
    e_middle = clean_all + e_piece[2] * e_merged
    e_norm_two, e_inverse_two = norm_parts(e_middle)
    e_two = (e_norm_two * (1.0 + e_piece[4]) + e_piece[3]).astype(BF)
    e_acts = dot(e_two, e_units)
    e_gate_act = e_acts[:, :unit]
    e_lift_act = e_acts[:, unit:]
    e_hidden = (jax.nn.silu(e_gate_act) * e_lift_act).astype(BF)
    e_lowered = noise.scatter_sum(token_blocks(dot(e_hidden, e_lower)))

    def own_part(value):
        return lax.dynamic_slice_in_dim(value, noise.me * own_rows, own_rows, 0)

    latent_own = own_part(e_middle) + own_part(e_piece[5]) * e_lowered
    latent_low = latent_own.astype(BF)
    latent_all = jnp.concatenate(noise.gather(latent_low)).astype(F32)

    sines = sinusoid(times, width).astype(BF).reshape(levels * images, width)
    temb = jnp.concatenate(noise.gather(dot(sines, d_time)), -1)
    cond = (
        latent_all.reshape(1, images, length, width)
        + temb.reshape(levels, images, 1, width)
    ).reshape(levels * rows, width)
    cond_low = jax.nn.silu(cond).astype(BF)
    mod = mod_dot(cond_low, d_mod)
    shift_one, scale_one, gate_one, shift_two, scale_two, gate_two = [
        mod[n * quarter : (n + 1) * quarter] for n in range(6)
    ]
    ratio = jnp.repeat(times.reshape(-1), length)[None]
    clean_up = lax.dynamic_slice_in_dim(clean_group.T, place, quarter, 0).astype(F32)
    noisy = (1.0 - ratio) * jnp.tile(clean_up, (1, levels)) + ratio * noise_cols.astype(F32)
    norm_one = (noisy - mean_one) * inverse_one
    one = (norm_one * (1.0 + scale_one) + shift_one).astype(BF)
    one_all, heads = join_dot(me, noise.near(one), d_att)
    mixed = attend_forward(heads, decoder_gains, length, True)
    mixed_all, merged = join_dot(me, noise.near(mixed), d_merge, True)
    middle = noisy + gate_one * merged
    part_mean = jnp.mean(middle, 0)
    part_center = middle - part_mean[None]
    part_square = jnp.sum(part_center * part_center, 0)
    parts = noise.near(jnp.stack([part_mean, part_square]))
    mean_two = sum(part[0] for part in parts) / noise_count
    square = sum(part[1] + quarter * (part[0] - mean_two) ** 2 for part in parts)
    inverse_two = lax.rsqrt(square / width + EPS)[None]
    norm_two = (middle - mean_two[None]) * inverse_two
    two = (norm_two * (1.0 + scale_two) + shift_two).astype(BF)
    two_all, acts, hidden = units_dot(me, noise.near(two), d_units)
    lowered = noise.near_sum(*lowered_dot(me, hidden, d_lower))
    output = (middle + gate_two * lowered).astype(BF)
    velocity = jnp.concatenate(
        noise.exchange(jnp.moveaxis(output.reshape(quarter, levels, rows), 1, 0))
    )
    velocity = velocity.T.reshape(1, images, length, width)

    def norm_back_cols(grad, normed, inverse):
        sums = noise.total(jnp.stack([jnp.sum(grad, 0), jnp.sum(grad * normed, 0)]))
        sums = sums[:, None] / width
        return inverse * (grad - sums[0] - normed * sums[1])

    low_cols = (cot_cols * gate_two).astype(BF)
    low_all, g_hidden = lower_back_dot(me, noise.near(low_cols), d_lower)
    g_gate_two = cot_cols * lowered
    g_acts, *given = acts_back(me, g_hidden, acts, d_units)
    g_two = noise.near_sum(*given)
    gw_lower = grad_dot(hidden, low_all, grad_low_kernel)
    gw_units = grad_dot(two_all, g_acts)
    g_middle = cot_cols + norm_back_cols(g_two * (1.0 + scale_two), norm_two, inverse_two)
    g_merged_low = (g_middle * gate_one).astype(BF)
    g_mixed = noise.near_sum(*spread_up_dot(me, g_merged_low, d_merge))
    gw_merge = grad_dot(mixed_all, g_merged_low, grad_turned_kernel)
    g_heads, d_gain_grad = attend_backward(
        g_mixed.astype(BF), decoder_gains, heads, length, True
    )
    g_one = noise.near_sum(*spread_dot(me, g_heads, d_att))
    gw_att = grad_dot(one_all, g_heads)
    g_noisy = g_middle + norm_back_cols(g_one * (1.0 + scale_one), norm_one, inverse_one)
    g_parts = (
        g_one,
        g_one * norm_one,
        g_middle * merged,
        g_two,
        g_two * norm_two,
        g_gate_two,
    )
    g_mod, g_cond_low = mod_back([part.astype(BF) for part in g_parts], d_mod)
    gw_mod = grad_dot(cond_low, g_mod, grad_low_kernel)
    g_cond = g_cond_low * silu_slope(cond)
    g_temb = noise.scatter_sum(
        column_blocks(jnp.sum(g_cond.reshape(levels * images, length, width), 1)), F32
    ).astype(BF)
    gw_time = dot_tn(sines, g_temb)
    g_latent = noise.scatter_sum(token_blocks(jnp.sum(g_cond.reshape(levels, rows, width), 0)))
    g_clean_cols = jnp.sum(
        ((1.0 - ratio) * g_noisy).reshape(quarter, levels, rows), 1
    ).astype(BF).T
    g_clean = jnp.concatenate(
        noise.exchange(g_clean_cols.reshape(noise_count, own_rows, quarter)), -1
    ).astype(F32)

    piece = [own_part(part) for part in e_piece]
    norm_two_own = own_part(e_norm_two)
    norm_one_own = own_part(e_norm_one)
    e_low_all = jnp.concatenate(noise.gather((g_latent * piece[5]).astype(BF)))
    e_g_gate_two = g_latent * e_lowered
    ew_lower = dot_tn(e_hidden, e_low_all)
    e_g_hidden = dot_nt(e_low_all, e_lower)
    e_g_gate_low = (e_g_hidden * e_lift_act * silu_slope(e_gate_act)).astype(BF)
    e_g_lift_low = (e_g_hidden * jax.nn.silu(e_gate_act)).astype(BF)
    e_g_acts = jnp.concatenate([e_g_gate_low, e_g_lift_low], -1)
    ew_units = dot_tn(e_two, e_g_acts)
    e_g_two = noise.scatter_sum(token_blocks(dot_nt(e_g_acts, e_units)))
    e_g_middle = g_latent + norm_back(
        e_g_two * (1.0 + piece[4]), norm_two_own, own_part(e_inverse_two)
    )
    e_merged_low = jnp.concatenate(noise.gather((e_g_middle * piece[2]).astype(BF)))
    e_merged_cols = columns(e_merged_low)
    ew_merge = dot_tn(e_mixed_all, e_merged_cols)
    e_g_mixed = noise.scatter_sum(column_blocks(dot_nt(e_merged_cols, e_merge)))
    e_g_heads, e_gain_grad = attend_backward(
        e_g_mixed.astype(BF), encoder_gains, e_heads, length
    )
    ew_att = dot_tn(e_one, e_g_heads)
    e_g_one = noise.scatter_sum(token_blocks(dot_nt(e_g_heads, e_att)))
    e_g_clean = e_g_middle + norm_back(
        e_g_one * (1.0 + piece[1]), norm_one_own, own_part(e_inverse_one)
    )
    clean_grad = (e_g_clean + g_clean).reshape(own_images, length, width)
    e_g_mod = jnp.concatenate(
        [
            e_g_one,
            e_g_one * norm_one_own,
            e_g_middle * own_part(e_merged),
            e_g_two,
            e_g_two * norm_two_own,
            e_g_gate_two,
        ],
        -1,
    )
    e_g_mod = jnp.sum(e_g_mod.reshape(own_images, length, -1), 1).astype(BF)
    every_mod = noise.exchange(
        jnp.moveaxis(e_g_mod.reshape(own_images, noise_count, -1), 1, 0)
    )
    every_mod = jnp.concatenate(every_mod)
    gains = noise.total(jnp.stack([e_gain_grad, d_gain_grad]))
    message = jnp.concatenate([every_mod.astype(F32).reshape(-1), gains.reshape(-1)])
    message = groups.gather_direct(message)
    every_mod, gain_total = message[:, : every_mod.size], message[:, every_mod.size :]
    every_mod = every_mod.astype(BF).reshape(-1, encoder_modulate.shape[1])
    gain_total = jnp.sum(gain_total, 0).reshape(gains.shape)
    grad_e_mod = dot_tn(class_low, every_mod)
    g_class = noise.total(dot_nt(every_mod, encoder_modulate)) * silu_slope(class_cond)
    grad_table = lax.dot_general(
        g_class,
        onehot.astype(F32),
        (((0,), (0,)), ((), ())),
        precision=lax.Precision.HIGHEST,
        preferred_element_type=F32,
    )

    def by_group(grad):
        low = grad.astype(BF)
        return low.reshape((groups_count, -1) + low.shape[1:])

    def finish_pieces(mine, pieces):
        mine = mine.astype(BF).reshape(mine.shape[0], pieces, quarter)
        came = jnp.stack(noise.exchange(return_pieces(noise, mine)))
        return join_pieces(noise, came, pieces).astype(F32)

    def finish_units(mine):
        came = jnp.stack(noise.exchange(return_units(noise, mine.astype(BF))))
        return join_units(noise, groups, came).astype(F32)

    def finish_lower(mine):
        mine = mine.astype(BF).reshape(-1, width)
        came = jnp.stack(noise.exchange(column_blocks(mine)))
        return came.reshape(-1, quarter).astype(F32)

    def finish(arrays, picked, e_or_d):
        kinds = tuple(e_or_d[n] for n in picked)
        full = (
            (chunk_rows, encoder_attend.shape[1]),
            (chunk_rows, unit),
            (chunk_rows, unit),
            encoder_lower.shape,
            (chunk_rows, encoder_modulate.shape[1]),
        )
        if groups.quick:
            return trade(
                noise,
                me,
                arrays,
                kinds,
                low_units,
                True,
                [full[n] for n in picked],
                F32,
            )
        ends = {"units": finish_units, "lower": finish_lower}
        return [
            finish_pieces(array, kind[1]) if kind[0] == "pieces" else ends[kind[0]](array)
            for array, kind in zip(arrays, kinds)
        ]

    d_second = groups.sum_whole(
        jnp.concatenate([by_group(gw_units), pad_lower(by_group(gw_lower))], 1)
    )
    grad_d_gate, grad_d_lift, grad_d_lower = finish(
        (
            d_second[:chunk_rows, :unit],
            d_second[:chunk_rows, unit:],
            d_second[chunk_rows:, :width],
        ),
        (1, 2, 3),
        d_kinds,
    )
    d_first = groups.sum_whole(
        jnp.concatenate([by_group(part) for part in [gw_mod, gw_att, gw_merge, gw_time]], -1)
    )
    grad_d_att, grad_d_mod = finish(
        (d_first[:, 6 * quarter : 9 * quarter], d_first[:, : 6 * quarter]), (0, 4), d_kinds
    )
    grad_d_merge = d_first[:, 9 * quarter : 10 * quarter]
    grad_time = d_first[:, 10 * quarter :]
    e_low_sum = groups.scatter_sum(by_group(ew_lower))
    e_second = groups.scatter_sum(
        by_group(ew_units)
    )
    e_first = groups.scatter_sum(
        jnp.concatenate([by_group(part) for part in [ew_att, ew_merge]], -1)
    )
    grad_e_att, grad_e_gate, grad_e_lift, grad_e_lower = finish(
        (e_first[:, : 3 * quarter], e_second[:, :unit], e_second[:, unit:], e_low_sum),
        (0, 1, 2, 3),
        e_kinds,
    )
    grad_e_merge = e_first[:, 3 * quarter :]
    return (
        velocity,
        latent_low.reshape(own_images, length, width),
        clean_grad,
        grad_e_mod,
        grad_e_att,
        grad_e_merge,
        grad_e_gate,
        grad_e_lift,
        grad_e_lower,
        grad_table,
        gain_total[0],
        grad_d_mod,
        grad_d_att,
        grad_d_merge,
        grad_d_gate,
        grad_d_lift,
        grad_d_lower,
        grad_time,
        gain_total[1],
    )


def solution(mesh):
    return jax.shard_map(
        functools.partial(per_device, mesh.shape["dp"], mesh.shape["noise"]),
        mesh=mesh,
        in_specs=(
            P(("dp", "noise"), None, None),
            P("noise", "dp", None, None),
            P("noise", "dp"),
            P(("dp", "noise")),
            P("noise", "dp", None, None),
            P("dp", "noise"),
            P("dp", "noise"),
            P("dp", "noise"),
            P("dp", "noise"),
            P("dp", "noise"),
            P("dp", "noise"),
            P("dp", "noise"),
            P(),
            P("dp", "noise"),
            P("dp", "noise"),
            P("dp", "noise"),
            P("dp", "noise"),
            P("dp", "noise"),
            P("dp", "noise"),
            P("dp", "noise"),
            P(),
        ),
        out_specs=(
            P("noise", "dp", None, None),
            P(("dp", "noise"), None, None),
            P(("dp", "noise"), None, None),
            P("dp", "noise"),
            P("dp", "noise"),
            P("dp", "noise"),
            P("dp", "noise"),
            P("dp", "noise"),
            P("dp", "noise"),
            P("dp", "noise"),
            P(),
            P("dp", "noise"),
            P("dp", "noise"),
            P("dp", "noise"),
            P("dp", "noise"),
            P("dp", "noise"),
            P("dp", "noise"),
            P("dp", "noise"),
            P(),
        ),
        check_vma=False,
    )
```

```python
import functools
import math

import jax
import jax.numpy as jnp
import numpy as np
from jax import lax
from jax.experimental import pallas as pl
from jax.experimental.pallas import tpu as pltpu
from jax.sharding import PartitionSpec as P

HEADS = 16
HEAD = 72
NT = 1000
GRID = 8


EPS = 1e-06


def angle_tables(length):
    places = np.arange(length)
    quarter = HEAD // 4
    freqs = np.exp(-math.log(10000.0) * np.arange(quarter) / quarter)
    row_angle = (places // GRID)[:, None] * freqs[None, :]
    col_angle = (places % GRID)[:, None] * freqs[None, :]
    return (row_angle, col_angle)


def sinusoid(times, width):
    half = width // 2
    freqs = jnp.exp(-math.log(10000.0) * jnp.arange(half).astype(jnp.float32) / half)
    angle = (times * 1000.0)[..., None] * freqs
    return jnp.concatenate([jnp.cos(angle), jnp.sin(angle)], -1)


BF = jnp.bfloat16
F32 = jnp.float32


def dot(left, right):
    return jnp.dot(left, right, preferred_element_type=F32)


def dot_nt(left, right):
    return lax.dot_general(left, right, (((1,), (1,)), ((), ())), preferred_element_type=F32)


def dot_tn(left, right):
    return lax.dot_general(left, right, (((0,), (0,)), ((), ())), preferred_element_type=F32)


def dot_tt(left, right):
    return lax.dot_general(left, right, (((0,), (1,)), ((), ())), preferred_element_type=F32)


def pick(array, index, axis=0):
    return lax.dynamic_index_in_dim(array, index, axis, keepdims=False)


class Noise:
    def __init__(self, count):
        self.count = count
        self.me = lax.axis_index("noise")
        self.quick = count == 4

    def swap(self, array, mask):
        return lax.ppermute(array, "noise", [(n, n ^ mask) for n in range(self.count)])

    def order(self, near):
        odd = self.me % 2 == 1
        far = self.me // 2 == 1
        near = [
            jnp.where(odd, near[1], near[0]),
            jnp.where(odd, near[0], near[1]),
            jnp.where(odd, near[3], near[2]),
            jnp.where(odd, near[2], near[3]),
        ]
        return [
            jnp.where(far, near[2], near[0]),
            jnp.where(far, near[3], near[1]),
            jnp.where(far, near[0], near[2]),
            jnp.where(far, near[1], near[3]),
        ]

    def gather(self, array):
        if not self.quick:
            whole = lax.all_gather(array, "noise", axis=0, tiled=False)
            return [whole[n] for n in range(self.count)]
        across = self.swap(array, 2)
        beside = self.swap(array, 1)
        corner = self.swap(across, 1)
        return self.order([array, beside, across, corner])

    def near(self, array):
        across = self.swap(array, 2)
        beside = self.swap(array, 1)
        return [array, beside, across, self.swap(across, 1)]

    def near_sum(self, keep, send):
        half = keep.astype(F32) + self.swap(send, 1).astype(F32)
        return half[0] + self.swap(half[1].astype(BF), 2).astype(F32)

    def scatter_sum(self, blocks, wire=BF):
        if not self.quick:
            return lax.psum_scatter(
                blocks.astype(wire), "noise", scatter_dimension=0, tiled=False
            ).astype(F32)
        core = self.me % 2
        far = self.me // 2
        pairs = blocks.reshape((2, 2) + blocks.shape[1:])
        keep = pick(pairs, core, 1).astype(F32)
        send = pick(pairs, 1 - core, 1).astype(wire)
        half = keep + self.swap(send, 1).astype(F32)
        return pick(half, far) + self.swap(pick(half, 1 - far).astype(wire), 2).astype(F32)

    def total(self, array):
        if not self.quick:
            return lax.psum(array, "noise")
        array = array + self.swap(array, 1)
        return array + self.swap(array, 2)

    def exchange(self, blocks):
        if not self.quick:
            whole = lax.all_to_all(blocks, "noise", 0, 0)
            return [whole[n] for n in range(self.count)]
        near = [pick(blocks, self.me)]
        for mask in (1, 2, 3):
            near.append(self.swap(pick(blocks, self.me ^ mask), mask))
        return self.order(near)


class Groups:
    def __init__(self, count):
        self.count = count
        self.quick = count == 8
        self.sides = 2
        self.line = count // 2
        self.place = lax.axis_index("dp")
        self.spot = self.place // self.sides
        self.side = self.place % self.sides
        self.across = [
            (z * 2 + x, z * 2 + 1 - x) for z in range(self.line) for x in range(2)
        ]

    def shift(self, array, spots, step):
        pairs = [(z * 2 + x, (z + step) * 2 + x) for z in spots for x in range(2)]
        return lax.ppermute(array, "dp", pairs)

    def turn(self, array, step):
        pairs = [
            (z * 2 + x, (z + step) % self.line * 2 + x)
            for z in range(self.line)
            for x in range(2)
        ]
        return lax.ppermute(array, "dp", pairs)

    def swap(self, array, mask):
        return lax.ppermute(array, "dp", [(n, n ^ mask) for n in range(self.count)])

    def gather_whole(self, array):
        return lax.all_gather(array, "dp", axis=0, tiled=False)

    def sum_whole(self, blocks):
        return lax.psum_scatter(
            blocks.astype(BF), "dp", scatter_dimension=0, tiled=False
        ).astype(F32)

    def gather(self, array):
        if not self.quick:
            return self.gather_whole(array), array
        near = [array] + [self.turn(array, step) for step in (1, 2, 3)]
        far = [lax.ppermute(part, "dp", self.across) for part in near]
        return place_blocks(self.place.reshape(1), near + far), near[3]

    def scatter_sum(self, blocks, wire=BF):
        if not self.quick:
            return self.sum_whole(blocks)
        pairs = blocks.reshape((self.line, 2) + blocks.shape[1:])
        keep = pick(pairs, self.side, 1).astype(F32)
        send = pick(pairs, 1 - self.side, 1).astype(wire)
        half = keep + lax.ppermute(send, "dp", self.across).astype(F32)
        total = pick(half, self.spot)
        for step in (1, 3, 2):
            part = pick(half, (self.spot + step) % self.line).astype(wire)
            total = total + self.turn(part, step).astype(F32)
        return total

    def gather_small(self, array):
        if not self.quick:
            return self.gather_whole(array)
        array = array[None]
        for mask in (1, 2, 4):
            other = self.swap(array, mask)
            high = (self.place // mask) % 2 == 1
            array = jnp.where(
                high, jnp.concatenate([other, array]), jnp.concatenate([array, other])
            )
        return array

    def gather_direct(self, array):
        if not self.quick:
            return self.gather_whole(array)
        came = [array]
        for step in range(1, self.count):
            pairs = [(n, (n + step) % self.count) for n in range(self.count)]
            came.append(lax.ppermute(array, "dp", pairs))
        turned = jnp.stack((came + came)[::-1])
        return lax.dynamic_slice_in_dim(turned, self.count - 1 - self.place, self.count, 0)

    def sum_small(self, blocks):
        if not self.quick:
            return lax.psum_scatter(blocks, "dp", scatter_dimension=0, tiled=False)
        for mask in (4, 2, 1):
            halves = blocks.reshape((2, -1) + blocks.shape[1:])
            high = (self.place // mask) % 2
            blocks = pick(halves, high) + self.swap(pick(halves, 1 - high), mask)
        return blocks[0]

    def total(self, array):
        if not self.quick:
            return lax.psum(array, "dp")
        for mask in (1, 2, 4):
            array = array + self.swap(array, mask)
        return array


def split_pieces(noise, weight, pieces):
    count = noise.count
    rows, width = weight.shape
    chunk = width // pieces
    slots = -(-pieces // count)
    parts = jnp.moveaxis(weight.reshape(rows, pieces, chunk), 1, 0)
    parts = jnp.concatenate(
        [parts, jnp.zeros((slots * count - pieces, rows, chunk), weight.dtype)]
    ).reshape(slots, count, rows, chunk)
    parts = jnp.roll(parts, pieces * noise.me, axis=1)
    return jnp.moveaxis(parts, 1, 0)


def take_pieces(noise, came, pieces):
    count = noise.count
    out = []
    for piece in range(pieces):
        chunk = count * piece + noise.me
        out.append(came[chunk // pieces, (chunk % pieces) // count])
    return jnp.stack(out, 1)


def return_pieces(noise, grad):
    count = noise.count
    pieces = grad.shape[1]
    slots = -(-pieces // count)
    rows = []
    for target in range(count):
        first = (noise.me - pieces * target) % count
        line = []
        for slot in range(slots):
            turn = jnp.minimum(first + slot * count, pieces - 1)
            line.append(pick(grad, (pieces * target + turn) // count, 1))
        rows.append(jnp.stack(line))
    return jnp.stack(rows)


def join_pieces(noise, came, pieces):
    count = noise.count
    out = []
    for turn in range(pieces):
        chunk = pieces * noise.me + turn
        out.append(came[chunk % count, turn // count])
    joined = jnp.stack(out, 1)
    return joined.reshape(joined.shape[0], -1)


def split_units(noise, groups, weight):
    count = noise.count
    rows, width = weight.shape
    low = groups.count // count
    parts = weight.reshape(rows, low, count, width // (low * count))
    return parts.transpose(2, 0, 1, 3).reshape(count, rows, width // count)


def take_units(noise, groups, came):
    count, rows, width = came.shape
    return jnp.moveaxis(came, 0, 1).reshape(rows, count * width)


def return_units(noise, grad):
    rows, width = grad.shape
    return jnp.moveaxis(grad.reshape(rows, noise.count, width // noise.count), 1, 0)


def join_units(noise, groups, came):
    count, rows, width = came.shape
    low = groups.count // count
    parts = came.reshape(count, rows, low, width // low)
    return parts.transpose(1, 2, 0, 3).reshape(rows, count * width)


def place_weights(noise, groups, w_att, w_gate, w_lift, w_lower, w_mod=None):
    rows = w_att.shape[0]
    att = split_pieces(noise, w_att, 3)
    chunk = att.shape[-1]
    parts = [att.reshape(noise.count, rows, chunk)]
    if w_mod is not None:
        mod = split_pieces(noise, w_mod, 6)
        parts += [mod[:, 0], mod[:, 1]]
    parts.append(split_units(noise, groups, w_gate))
    parts.append(split_units(noise, groups, w_lift))
    unit = parts[-1].shape[-1]
    parts.append(w_lower.reshape(noise.count, rows, unit))
    came = jnp.stack(noise.exchange(jnp.concatenate(parts, -1)))
    spot = 0
    out = [take_pieces(noise, came[:, None, :, :chunk], 3)]
    spot = chunk
    if w_mod is not None:
        mod = jnp.stack([came[:, :, chunk : 2 * chunk], came[:, :, 2 * chunk : 3 * chunk]], 1)
        out.append(take_pieces(noise, mod, 6))
        spot = 3 * chunk
    out.append(take_units(noise, groups, came[:, :, spot : spot + unit]))
    spot += unit
    out.append(take_units(noise, groups, came[:, :, spot : spot + unit]))
    spot += unit
    lower = came[:, :, spot:].reshape(noise.count, -1, w_lower.shape[1])
    lower = jnp.moveaxis(lower, 0, 1)
    out.append(lower.reshape(lower.shape[0], -1))
    return out


def flat(weight):
    return weight.reshape(weight.shape[0] * weight.shape[1], -1)


def norm_parts(value):
    mean = jnp.mean(value, -1, keepdims=True)
    center = value - mean
    inverse = lax.rsqrt(jnp.mean(center * center, -1, keepdims=True) + EPS)
    return center * inverse, inverse


def norm_back(grad, normed, inverse):
    first = jnp.mean(grad, -1, keepdims=True)
    second = jnp.mean(grad * normed, -1, keepdims=True)
    return inverse * (grad - first - normed * second)


def silu_slope(value):
    gate = jax.nn.sigmoid(value)
    return gate * (1.0 + value * (1.0 - gate))


VMEM_BYTES = 48 * 1024 * 1024
STEP = 256


def kernel_call(kernel, grid, ins, outs, scratch=(), scalars=1):
    return pl.pallas_call(
        kernel,
        out_shape=[shape for shape, _ in outs],
        grid_spec=pltpu.PrefetchScalarGridSpec(
            num_scalar_prefetch=scalars,
            grid=grid,
            in_specs=ins,
            out_specs=[spec for _, spec in outs],
            scratch_shapes=list(scratch),
        ),
        compiler_params=pltpu.CompilerParams(vmem_limit_bytes=VMEM_BYTES),
    )


def row_spec(width):
    return pl.BlockSpec((STEP, width), lambda n, *_: (n, 0))


def up_spec(width):
    return pl.BlockSpec((width, STEP), lambda n, *_: (0, n))


def full_spec(shape):
    return pl.BlockSpec(shape, lambda n, *_: (0,) * len(shape))


def shaped(shape, dtype):
    return jax.ShapeDtypeStruct(shape, dtype)


def joined(me_ref, near, parts):
    for n, ref in enumerate(near):
        parts[me_ref[0] ^ n] = ref[...]
    return jnp.concatenate([parts[n] for n in range(4)])


def near_scratch(near):
    return [pltpu.VMEM((4, near[0].shape[0], STEP), BF)]


def place_kernel(place_ref, *refs):
    blocks, out_ref, sems = refs[:8], refs[8], refs[9]
    spot, side = place_ref[0] // 2, place_ref[0] % 2
    copies = []
    for n, ref in enumerate(blocks):
        line = (spot + 4 - n % 4) % 4
        at = line * 2 + (side if n < 4 else 1 - side)
        copies.append(pltpu.make_async_copy(ref, out_ref.at[at], sems.at[n]))
    for copy in copies:
        copy.start()
    for copy in copies:
        copy.wait()


def place_blocks(place, blocks):
    block = blocks[0]
    return pl.pallas_call(
        place_kernel,
        out_shape=shaped((len(blocks),) + block.shape, block.dtype),
        in_specs=[pl.BlockSpec(memory_space=pltpu.SMEM)]
        + [pl.BlockSpec(memory_space=pl.ANY)] * len(blocks),
        out_specs=pl.BlockSpec(memory_space=pl.ANY),
        scratch_shapes=[pltpu.SemaphoreType.DMA((len(blocks),))],
        compiler_params=pltpu.CompilerParams(vmem_limit_bytes=8 * 1024 * 1024),
    )(place, *blocks)


def join_kernel(upward, me_ref, x0, x1, x2, x3, w_ref, full_ref, out_ref, parts):
    whole = joined(me_ref, (x0, x1, x2, x3), parts)
    full_ref[...] = whole
    if upward:
        out_ref[...] = dot_tn(w_ref[...], whole)
    else:
        out_ref[...] = dot_tn(whole, w_ref[...])


def join_dot(me, near, weight, upward=False):
    quarter, rows = near[0].shape
    width = weight.shape[1]
    if upward:
        out = (shaped((width, rows), F32), up_spec(width))
    else:
        out = (shaped((rows, width), F32), row_spec(width))
    return kernel_call(
        functools.partial(join_kernel, upward),
        (rows // STEP,),
        [up_spec(quarter)] * 4 + [full_spec(weight.shape)],
        [(shaped((4 * quarter, rows), BF), up_spec(4 * quarter)), out],
        near_scratch(near),
    )(me, *near, weight)


def rows_spec(weight, depth):
    if weight.ndim == 2:
        return full_spec(weight.shape)
    count = weight.shape[0]
    return pl.BlockSpec((count, depth // count, weight.shape[2]), lambda n, *_: (0, 0, 0))


def rows_part(ref, n, parts):
    size = ref.shape[0] // parts
    part = ref[n * size : (n + 1) * size]
    return part.reshape(-1, part.shape[-1])


def units_kernel(me_ref, x0, x1, x2, x3, w_ref, full_ref, out_ref, hid_ref, parts):
    whole = joined(me_ref, (x0, x1, x2, x3), parts)
    full_ref[...] = whole
    acts = dot_tn(whole, rows_part(w_ref, 0, 1))
    out_ref[...] = acts
    unit = hid_ref.shape[1]
    hid_ref[...] = (jax.nn.silu(acts[:, :unit]) * acts[:, unit:]).astype(BF)


def units_dot(me, near, weight):
    quarter, rows = near[0].shape
    width = weight.shape[-1]
    return kernel_call(
        units_kernel,
        (rows // STEP,),
        [up_spec(quarter)] * 4 + [rows_spec(weight, 4 * quarter)],
        [
            (shaped((4 * quarter, rows), BF), up_spec(4 * quarter)),
            (shaped((rows, width), F32), row_spec(width)),
            (shaped((rows, width // 2), BF), row_spec(width // 2)),
        ],
        near_scratch(near),
    )(me, *near, weight)


def lower_kernel(me_ref, x0, x1, x2, x3, w_ref, full_ref, out_ref, parts):
    whole = joined(me_ref, (x0, x1, x2, x3), parts).T
    full_ref[...] = whole
    out_ref[...] = dot_nt(whole, w_ref[...])


def lower_back_dot(me, near, weight):
    quarter, rows = near[0].shape
    width = weight.shape[0]
    return kernel_call(
        lower_kernel,
        (rows // STEP,),
        [up_spec(quarter)] * 4 + [full_spec(weight.shape)],
        [
            (shaped((rows, 4 * quarter), BF), row_spec(4 * quarter)),
            (shaped((rows, width), F32), row_spec(width)),
        ],
        near_scratch(near),
    )(me, *near, weight)


def give(parts, keep_ref, send_ref):
    keep_ref[0] = parts[0]
    keep_ref[1] = parts[2]
    send_ref[0] = parts[1]
    send_ref[1] = parts[3]


def give_outs(rows, quarter):
    pair = pl.BlockSpec((2, quarter, STEP), lambda n, *_: (0, 0, n))
    return [(shaped((2, quarter, rows), BF), pair)] * 2


def spread_kernel(me_ref, y_ref, w_ref, keep_ref, send_ref, parts):
    quarter = keep_ref.shape[1]
    value = y_ref[...]
    for n in range(4):
        term = dot_nt(w_ref[n * quarter : (n + 1) * quarter], value)
        parts[me_ref[0] ^ n] = term.astype(BF)
    give(parts, keep_ref, send_ref)


def spread_dot(me, value, weight):
    rows, width = value.shape
    quarter = weight.shape[0] // 4
    return kernel_call(
        spread_kernel,
        (rows // STEP,),
        [row_spec(width), full_spec(weight.shape)],
        give_outs(rows, quarter),
        [pltpu.VMEM((4, quarter, STEP), BF)],
    )(me, value, weight)


def spread_up_kernel(me_ref, y_ref, w_ref, keep_ref, send_ref, parts):
    quarter = keep_ref.shape[1]
    value = y_ref[...]
    for n in range(4):
        term = dot(w_ref[n * quarter : (n + 1) * quarter], value)
        parts[me_ref[0] ^ n] = term.astype(BF)
    give(parts, keep_ref, send_ref)


def spread_up_dot(me, value, weight):
    width, rows = value.shape
    quarter = weight.shape[0] // 4
    return kernel_call(
        spread_up_kernel,
        (rows // STEP,),
        [up_spec(width), full_spec(weight.shape)],
        give_outs(rows, quarter),
        [pltpu.VMEM((4, quarter, STEP), BF)],
    )(me, value, weight)


def lowered_kernel(me_ref, y_ref, w_ref, keep_ref, send_ref, parts):
    quarter = keep_ref.shape[1]
    term = dot(y_ref[...], w_ref[...]).astype(BF).T
    for n in range(4):
        parts[me_ref[0] ^ n] = term[n * quarter : (n + 1) * quarter]
    give(parts, keep_ref, send_ref)


def lowered_dot(me, value, weight):
    rows, width = value.shape
    quarter = weight.shape[1] // 4
    return kernel_call(
        lowered_kernel,
        (rows // STEP,),
        [row_spec(width), full_spec(weight.shape)],
        give_outs(rows, quarter),
        [pltpu.VMEM((4, quarter, STEP), BF)],
    )(me, value, weight)


def acts_back_kernel(me_ref, g_ref, a_ref, w_ref, acts_ref, keep_ref, send_ref, parts):
    quarter = keep_ref.shape[1]
    unit = g_ref.shape[1]
    grad = g_ref[...]
    gate_act, lift_act = a_ref[:, :unit], a_ref[:, unit:]
    gate = jax.nn.sigmoid(gate_act)
    slope = gate * (1.0 + gate_act * (1.0 - gate))
    acts_ref[:, :unit] = (grad * lift_act * slope).astype(BF)
    acts_ref[:, unit:] = (grad * (gate_act * gate)).astype(BF)
    value = acts_ref[...]
    for n in range(4):
        term = dot_nt(rows_part(w_ref, n, 4), value)
        parts[me_ref[0] ^ n] = term.astype(BF)
    give(parts, keep_ref, send_ref)


def acts_back(me, grad, acts, weight, quarter):
    rows, unit = grad.shape
    return kernel_call(
        acts_back_kernel,
        (rows // STEP,),
        [row_spec(unit), row_spec(2 * unit), rows_spec(weight, 4 * quarter)],
        [(shaped((rows, 2 * unit), BF), row_spec(2 * unit))] + give_outs(rows, quarter),
        [pltpu.VMEM((4, quarter, STEP), BF)],
    )(me, grad, acts, weight)


def grad_kernel(x_ref, y_ref, out_ref):
    out_ref[...] = dot(x_ref[...], y_ref[...]).astype(BF)


def grad_turned_kernel(x_ref, y_ref, out_ref):
    out_ref[...] = dot_nt(x_ref[...], y_ref[...]).astype(BF)


def grad_low_kernel(x_ref, y_ref, out_ref):
    out_ref[...] = dot_tn(x_ref[...], y_ref[...]).astype(BF)


def grad_dot(left, right, kernel=grad_kernel):
    step = 384
    low = kernel is grad_low_kernel
    width, rows = left.shape[::-1] if low else left.shape
    wide = right.shape[0] if kernel is grad_turned_kernel else right.shape[1]
    if low:
        spec = pl.BlockSpec((rows, step), lambda n: (0, n))
    else:
        spec = pl.BlockSpec((step, rows), lambda n: (n, 0))
    return pl.pallas_call(
        kernel,
        out_shape=shaped((width, wide), BF),
        grid=(width // step,),
        in_specs=[spec, pl.BlockSpec(right.shape, lambda n: (0, 0))],
        out_specs=pl.BlockSpec((step, wide), lambda n: (n, 0)),
        compiler_params=pltpu.CompilerParams(vmem_limit_bytes=VMEM_BYTES),
    )(left, right)


def mod_kernel(x_ref, w_ref, out_ref):
    out_ref[...] = dot(x_ref[...], w_ref[...]).T[: out_ref.shape[0]]


def mod_spec(depth, wide):
    return pl.BlockSpec((depth, -(-wide // 128) * 128), lambda n, *_: (0, 0))


def mod_dot(value, weight, wide):
    rows, width = value.shape
    return kernel_call(
        mod_kernel,
        (rows // STEP,),
        [row_spec(width), mod_spec(width, wide)],
        [(shaped((wide, rows), F32), up_spec(wide))],
        scalars=0,
    )(value, weight)[0]


def mod_back_kernel(*refs):
    parts, (w_ref, cat_ref, out_ref) = refs[:6], refs[6:]
    grad = jnp.concatenate([ref[...] for ref in parts]).T
    cat_ref[...] = grad
    out_ref[...] = dot_nt(grad, w_ref[:, : grad.shape[1]])


def mod_back(parts, weight):
    quarter, rows = parts[0].shape
    width = weight.shape[0]
    return kernel_call(
        mod_back_kernel,
        (rows // STEP,),
        [up_spec(quarter)] * 6 + [mod_spec(width, 6 * quarter)],
        [
            (shaped((rows, 6 * quarter), BF), row_spec(6 * quarter)),
            (shaped((rows, width), F32), row_spec(width)),
        ],
        scalars=0,
    )(*parts, weight)


def kind_width(kind, quarter):
    if kind[0] == "pieces":
        return -(-kind[1] // 4) * quarter
    if kind[0] == "units":
        return kind[1] // 4
    return quarter


def pack_parts(me, kinds, low, quarter):
    out = []
    spot = 0
    for item, kind in enumerate(kinds):
        for far in range(4):
            to = me ^ far
            if kind[0] == "pieces":
                count = kind[1]
                for slot in range(-(-count // 4)):
                    turn = (to - count * me) % 4 + 4 * slot
                    if turn < count:
                        out.append(
                            (item, far, None, turn * quarter, spot + slot * quarter, quarter)
                        )
            elif kind[0] == "units":
                each = kind[1] // (4 * low)
                for n in range(low):
                    at = n * 4 * each + to * each
                    out.append((item, far, None, at, spot + n * each, each))
            else:
                out.append((item, far, (to * kind[1], kind[1]), 0, spot, quarter))
        spot += kind_width(kind, quarter)
    return out


def unpack_parts(me, kinds, low, quarter):
    out = []
    spot = 0
    for item, kind in enumerate(kinds):
        for far in range(4):
            come = me ^ far
            if kind[0] == "pieces":
                count = kind[1]
                for slot in range(-(-count // 4)):
                    turn = (me - count * come) % 4 + 4 * slot
                    if turn < count:
                        piece = (count * come + turn) // 4
                        out.append(
                            (item, far, None, piece * quarter, spot + slot * quarter, quarter)
                        )
            elif kind[0] == "units":
                each = kind[1] // (4 * low)
                for n in range(low):
                    at = (come * low + n) * each
                    out.append((item, far, None, at, spot + n * each, each))
            else:
                out.append((item, far, (0, kind[1]), come * quarter, spot, quarter))
        spot += kind_width(kind, quarter)
    return out


def pack_kernel(plan, me_ref, *refs):
    items, out_ref = refs[:-1], refs[-1]
    out_ref[...] = jnp.zeros_like(out_ref)
    for me in range(4):

        @pl.when(me_ref[0] == me)
        def _():
            for item, far, lines, at, spot, size in plan(me):
                first, count = lines or (0, out_ref.shape[1])
                out_ref[far, :count, spot : spot + size] = items[item][
                    first : first + count, at : at + size
                ].astype(BF)


def unpack_kernel(plan, me_ref, *refs):
    packets, outs = refs[:4], refs[4:]
    for me in range(4):

        @pl.when(me_ref[0] == me)
        def _():
            for item, far, lines, at, spot, size in plan(me):
                first, count = lines or (0, packets[0].shape[0])
                outs[item][first : first + count, at : at + size] = packets[far][
                    :count, spot : spot + size
                ].astype(outs[item].dtype)


def whole_call(kernel, outs, me, args):
    return kernel_call(
        kernel,
        (1,),
        [full_spec(arg.shape) for arg in args],
        [(out, full_spec(out.shape)) for out in outs],
    )(me, *args)


def trade(noise, me, arrays, kinds, low, back, shapes, dtype):
    quarter = kind_quarter(kinds, arrays, back)
    width = sum(kind_width(kind, quarter) for kind in kinds)
    lines = max(a.shape[0] for a, kind in zip(arrays, kinds) if kind[0] != "lower")
    there, here = (unpack_parts, pack_parts) if back else (pack_parts, unpack_parts)
    packed = whole_call(
        functools.partial(
            pack_kernel, functools.partial(there, kinds=kinds, low=low, quarter=quarter)
        ),
        [shaped((4, lines, width), BF)],
        me,
        arrays,
    )[0]
    near = [packed[0]] + [noise.swap(packed[n], n) for n in (1, 2, 3)]
    return whole_call(
        functools.partial(
            unpack_kernel, functools.partial(here, kinds=kinds, low=low, quarter=quarter)
        ),
        [shaped(shape, dtype) for shape in shapes],
        me,
        near,
    )


def kind_quarter(kinds, arrays, back):
    for array, kind in zip(arrays, kinds):
        if kind[0] == "pieces":
            return array.shape[1] // kind[1]
        if kind[0] == "lower":
            return array.shape[1] // 4 if back else array.shape[1]


def attend_tables(length, repeat, gains):
    heads = HEADS // 4
    row_angle, col_angle = angle_tables(length)
    angle = np.concatenate([row_angle, row_angle, col_angle, col_angle], -1)
    angle = np.tile(angle, (repeat, heads))
    spread = jnp.tile(gains, (1, heads))
    return jnp.asarray(np.cos(angle), F32), jnp.asarray(np.sin(angle), F32), spread


def attend_matrices():
    width = HEADS // 4 * HEAD
    quarter = HEAD // 4
    index = np.arange(width)
    same = (index[:, None] // HEAD == index[None, :] // HEAD).astype(np.float32)
    second = (index % (2 * quarter)) >= quarter
    source = np.where(second, index - quarter, index + quarter)
    turn = np.zeros((width, width), np.float32)
    turn[source, index] = np.where(second, 1.0, -1.0)
    low = jnp.asarray(same, BF), jnp.asarray(turn, BF), jnp.asarray(turn.T, BF)
    return low


def low_dot(value, matrix):
    return dot(value.astype(BF), matrix)


def head_masks(width):
    lane = lax.broadcasted_iota(jnp.int32, (1, width), 1)
    return [
        jnp.logical_and(lane >= n * HEAD, lane < (n + 1) * HEAD).astype(F32)
        for n in range(width // HEAD)
    ]


def ready_heads(value, gain, cosine, sine, same, turn):
    inverse = lax.rsqrt(low_dot(value * value, same) * (1.0 / HEAD) + EPS)
    normed = value * inverse
    scaled = normed * gain
    turned = scaled * cosine + low_dot(scaled, turn) * sine
    return turned.astype(BF), normed, inverse


def stack_heads(value, masks):
    value = value.astype(F32)
    return jnp.concatenate([value * mask for mask in masks]).astype(BF)


def fold_heads(value, masks, length):
    out = value[:length] * masks[0]
    for n in range(1, len(masks)):
        out = out + value[n * length : (n + 1) * length] * masks[n]
    return out


def prob_of(stacked, keys_low):
    scores = dot_nt(stacked, keys_low) * HEAD ** (-0.5)
    grown = jnp.exp(scores - jnp.max(scores, -1, keepdims=True))
    return grown / jnp.sum(grown, -1, keepdims=True)


def attend_kernel(
    length,
    upward,
    p_ref,
    cos_ref,
    sin_ref,
    gain_ref,
    same_ref,
    turn_ref,
    out_ref,
    mixed_ref,
):
    width = mixed_ref.shape[1]
    q_ref, k_ref, v_ref = [p_ref[:, n * width : (n + 1) * width] for n in range(3)]
    masks = head_masks(width)
    same, turn = same_ref[...], turn_ref[...]
    cosine, sine = cos_ref[...], sin_ref[...]
    query, _, _ = ready_heads(q_ref, gain_ref[0:1], cosine, sine, same, turn)
    key, _, _ = ready_heads(k_ref, gain_ref[1:2], cosine, sine, same, turn)
    value = v_ref.astype(BF)
    for image in range(mixed_ref.shape[0] // length):
        part = slice(image * length, (image + 1) * length)
        prob = prob_of(stack_heads(query[part], masks), key[part])
        mixed = dot(prob.astype(BF), value[part])
        mixed_ref[part] = fold_heads(mixed, masks, length)
    if upward:
        out_ref[...] = mixed_ref[...].T.astype(BF)
    else:
        out_ref[...] = mixed_ref[...].astype(BF)


def attend_back_kernel(
    length,
    upward,
    p_ref,
    cos_ref,
    sin_ref,
    gain_ref,
    same_ref,
    turn_ref,
    back_ref,
    grad_ref,
    dp_ref,
    dg_ref,
    gq_ref,
    gk_ref,
    gv_ref,
):
    width = gq_ref.shape[1]
    q_ref, k_ref, v_ref = [p_ref[:, n * width : (n + 1) * width] for n in range(3)]
    masks = head_masks(width)
    same, turn, back = same_ref[...], turn_ref[...], back_ref[...]
    cosine, sine = cos_ref[...], sin_ref[...]
    query, q_norm, q_inv = ready_heads(q_ref, gain_ref[0:1], cosine, sine, same, turn)
    key, k_norm, k_inv = ready_heads(k_ref, gain_ref[1:2], cosine, sine, same, turn)
    value = v_ref.astype(BF)
    grad = grad_ref[...].T if upward else grad_ref[...]
    for image in range(q_ref.shape[0] // length):
        part = slice(image * length, (image + 1) * length)
        stacked = stack_heads(query[part], masks)
        prob = prob_of(stacked, key[part])
        grads = stack_heads(grad[part], masks)
        gv_ref[part] = dot_tn(prob.astype(BF), grads)
        g_prob = dot_nt(grads, value[part])
        g_score = prob * (g_prob - jnp.sum(g_prob * prob, -1, keepdims=True))
        g_score = g_score.astype(BF)
        gq_ref[part] = fold_heads(dot(g_score, key[part]), masks, length)
        gk_ref[part] = dot_tn(g_score, stacked)

    @pl.when(pl.program_id(0) == 0)
    def _():
        dg_ref[...] = jnp.zeros_like(dg_ref)

    for n, (g_ref, normed, inverse) in enumerate(
        ((gq_ref, q_norm, q_inv), (gk_ref, k_norm, k_inv))
    ):
        turned = g_ref[...] * HEAD ** (-0.5)
        scaled = turned * cosine + low_dot(turned * sine, back)
        dg_ref[n : n + 1] += jnp.sum(scaled * normed, 0, keepdims=True)
        weighed = scaled * gain_ref[n : n + 1]
        mean = low_dot(weighed * normed, same) * (1.0 / HEAD)
        out = inverse * (weighed - normed * mean)
        dp_ref[:, n * width : (n + 1) * width] = out.astype(BF)
    dp_ref[:, 2 * width :] = gv_ref[...].astype(BF)


def attend_blocks(rows, length, width):
    step = STEP

    def row(size):
        return pl.BlockSpec((step, size), lambda n: (n, 0))

    def whole(*shape):
        return pl.BlockSpec(shape, lambda n: (0, 0))

    return step, row, whole


def attend_forward(project, gains, length, upward=False):
    rows, width = project.shape[0], project.shape[1] // 3
    step, row, whole = attend_blocks(rows, length, width)
    cosine, sine, spread = attend_tables(length, step // length, gains)
    same, turn, _ = attend_matrices()
    return pl.pallas_call(
        functools.partial(attend_kernel, length, upward),
        out_shape=shaped((width, rows) if upward else (rows, width), BF),
        grid=(rows // step,),
        in_specs=[row(3 * width), whole(step, width), whole(step, width), whole(2, width)]
        + [whole(width, width)] * 2,
        out_specs=up_spec(width) if upward else row(width),
        scratch_shapes=[pltpu.VMEM((step, width), F32)],
        compiler_params=pltpu.CompilerParams(vmem_limit_bytes=VMEM_BYTES),
    )(project, cosine, sine, spread, same, turn)


def attend_backward(grad_low, gains, project, length, upward=False):
    rows, width = project.shape[0], project.shape[1] // 3
    step, row, whole = attend_blocks(rows, length, width)
    cosine, sine, spread = attend_tables(length, step // length, gains)
    same, turn, back = attend_matrices()
    grad, gain_grad = pl.pallas_call(
        functools.partial(attend_back_kernel, length, upward),
        out_shape=(shaped((rows, 3 * width), BF), shaped((2, width), F32)),
        grid=(rows // step,),
        in_specs=[row(3 * width), whole(step, width), whole(step, width), whole(2, width)]
        + [whole(width, width)] * 3
        + [up_spec(width) if upward else row(width)],
        out_specs=(row(3 * width), whole(2, width)),
        scratch_shapes=[pltpu.VMEM((step, width), F32)] * 3,
        compiler_params=pltpu.CompilerParams(vmem_limit_bytes=VMEM_BYTES),
    )(project, cosine, sine, spread, same, turn, back, grad_low)
    return grad, jnp.sum(gain_grad.reshape(2, width // HEAD, HEAD), 1)


def per_device(
    groups_count,
    noise_count,
    clean_tokens,
    noise_tokens,
    time_index,
    class_label,
    velocity_cotangent,
    encoder_modulate,
    encoder_attend,
    encoder_merge,
    encoder_gate,
    encoder_lift,
    encoder_lower,
    class_table,
    encoder_gains,
    decoder_modulate,
    decoder_attend,
    decoder_merge,
    decoder_gate,
    decoder_lift,
    decoder_lower,
    time_weight,
    decoder_gains,
):
    noise = Noise(noise_count)
    groups = Groups(groups_count)
    own_images, length, width = clean_tokens.shape
    images = own_images * noise_count
    levels = noise_count
    quarter = width // noise_count
    own_rows = own_images * length
    rows = images * length
    place = noise.me * quarter

    def columns(value):
        return lax.dynamic_slice_in_dim(value, place, quarter, value.ndim - 1)

    def column_blocks(value):
        return jnp.moveaxis(value.reshape(value.shape[0], noise_count, quarter), 1, 0)

    def token_blocks(value):
        return value.reshape(noise_count, own_rows, width)

    facts = jnp.concatenate([class_label, time_index[0]])
    facts = jnp.stack(noise.gather(facts))
    times = (facts[:, own_images:].astype(F32) + 0.5) / NT
    labels = groups.gather_small(facts[:, :own_images].reshape(-1)).reshape(-1)

    me = noise.me.reshape(1)
    unit = encoder_gate.shape[1]
    chunk_rows = encoder_attend.shape[0]
    lower_rows = encoder_lower.shape[0] // noise_count
    low_units = groups_count // noise_count
    e_kinds = (("pieces", 3), ("units", unit), ("units", unit), ("lower", lower_rows))
    d_kinds = e_kinds + (("pieces", 6),)
    shapes = ((chunk_rows, 3 * quarter), (chunk_rows, unit), (chunk_rows, unit))
    shapes += ((lower_rows, width), (chunk_rows, 6 * quarter))
    if groups.quick:
        e_att_s, e_gate_s, e_lift_s, e_lower_s = trade(
            noise,
            me,
            (encoder_attend, encoder_gate, encoder_lift, encoder_lower),
            e_kinds,
            low_units,
            False,
            shapes[:4],
            BF,
        )
    else:
        e_att_s, e_gate_s, e_lift_s, e_lower_s = place_weights(
            noise, groups, encoder_attend, encoder_gate, encoder_lift, encoder_lower
        )
    (
        e_att_s,
        e_gate_s,
        e_lift_s,
        e_lower_s,
        clean_tokens,
        noise_tokens,
        velocity_cotangent,
        decoder_attend,
        decoder_gate,
    ) = lax.optimization_barrier(
        (
            e_att_s,
            e_gate_s,
            e_lift_s,
            e_lower_s,
            clean_tokens,
            noise_tokens,
            velocity_cotangent,
            decoder_attend,
            decoder_gate,
        )
    )
    e_first, early = groups.gather(
        jnp.concatenate([e_att_s.reshape(chunk_rows, -1), encoder_merge], -1)
    )
    labels, early = lax.optimization_barrier((labels, early))

    here = class_table.shape[1]
    onehot = (
        labels[:, None] == (jnp.arange(here) + noise.me * here)[None, :]
    ).astype(BF)
    class_cond = noise.total(dot_nt(onehot, class_table))
    class_low = jax.nn.silu(class_cond).astype(BF)
    class_mod = dot(class_low, encoder_modulate)
    class_mod = groups.sum_small(
        class_mod.reshape(groups_count, images, class_mod.shape[1])
    )
    class_mod = jnp.concatenate(noise.gather(class_mod), -1)

    e_att = flat(e_first[:, :, : 3 * quarter])
    e_merge = flat(e_first[:, :, 3 * quarter :])
    e_second_s, _, _ = lax.optimization_barrier(
        (jnp.concatenate([e_gate_s, e_lift_s], -1), early, class_low)
    )
    e_pair, later = groups.gather(e_second_s)
    e_units = flat(e_pair)
    e_lower_s, _, class_mod = lax.optimization_barrier((e_lower_s, later, class_mod))
    e_lower = flat(groups.gather(e_lower_s)[0])
    if groups.quick:
        d_att_s, d_gate_s, d_lift_s, d_lower_s, d_mod_s = trade(
            noise,
            me,
            (decoder_attend, decoder_gate, decoder_lift, decoder_lower, decoder_modulate),
            d_kinds,
            low_units,
            False,
            shapes,
            BF,
        )
    else:
        d_att_s, d_mod_s, d_gate_s, d_lift_s, d_lower_s = place_weights(
            noise,
            groups,
            decoder_attend,
            decoder_gate,
            decoder_lift,
            decoder_lower,
            decoder_modulate,
        )
    d_first_s = jnp.concatenate(
        [
            d_mod_s.reshape(chunk_rows, -1),
            jnp.zeros((chunk_rows, -6 * quarter % 128), BF),
            d_att_s.reshape(chunk_rows, -1),
            decoder_merge,
            time_weight,
        ],
        -1,
    )

    def pad_lower(part):
        ends = ((0, 0),) * (part.ndim - 1) + ((0, 2 * unit - width),)
        return jnp.pad(part, ends)

    d_second_s = jnp.concatenate(
        [jnp.concatenate([d_gate_s, d_lift_s], -1), pad_lower(d_lower_s)]
    )
    d_first_s, _, _, _ = lax.optimization_barrier((d_first_s, e_first, e_units, e_lower))
    d_whole = flat(groups.gather_whole(d_first_s))
    after = -(-6 * quarter // 128) * 128
    d_att, d_merge, d_time = [
        d_whole[:, after + first * quarter : after + last * quarter]
        for first, last in ((0, 3), (3, 4), (4, 5))
    ]
    clean_group = jnp.concatenate(noise.gather(clean_tokens.reshape(own_rows, width)))
    clean_all = clean_group.astype(F32)
    own_times = (time_index[0].astype(F32) + 0.5) / NT
    own_ratio = jnp.repeat(own_times, length)[:, None]
    own_noise = noise_tokens[0].reshape(rows, width)
    own_cot = velocity_cotangent[0].reshape(rows, width)
    own_noisy = (1.0 - own_ratio) * clean_all + own_ratio * own_noise.astype(F32)
    own_mean = jnp.mean(own_noisy, -1)
    own_center = own_noisy - own_mean[:, None]
    own_inverse = lax.rsqrt(jnp.mean(own_center * own_center, -1) + EPS)
    stats = jnp.stack(noise.gather(jnp.stack([own_mean, own_inverse])))
    mean_one = stats[:, 0].reshape(1, -1)
    inverse_one = stats[:, 1].reshape(1, -1)
    came = noise.exchange(
        jnp.stack(
            [
                own_noise.T.reshape(noise_count, quarter, rows),
                own_cot.T.reshape(noise_count, quarter, rows),
            ],
            1,
        )
    )
    noise_cols = jnp.concatenate([part[0] for part in came], -1)
    cot_cols = jnp.concatenate([part[1] for part in came], -1).astype(F32)

    e_piece = [
        jnp.repeat(part, length, axis=0) for part in jnp.split(class_mod, 6, axis=-1)
    ]
    e_norm_one, e_inverse_one = norm_parts(clean_all)
    e_one = (e_norm_one * (1.0 + e_piece[1]) + e_piece[0]).astype(BF)
    e_heads = dot(e_one, e_att)
    e_mixed = attend_forward(e_heads, encoder_gains, length)
    e_mixed, d_second_s = lax.optimization_barrier((e_mixed, d_second_s))
    d_pair = groups.gather_whole(d_second_s)
    d_units = d_pair if groups.quick else flat(d_pair[:, :chunk_rows])
    d_lower = flat(d_pair[:, chunk_rows:, :width])
    e_mixed_all = jnp.concatenate(noise.gather(e_mixed), -1)
    e_merged = jnp.concatenate(
        noise.gather(dot(e_mixed_all, e_merge).astype(BF)), -1
    ).astype(F32)
    e_middle = clean_all + e_piece[2] * e_merged
    e_norm_two, e_inverse_two = norm_parts(e_middle)
    e_two = (e_norm_two * (1.0 + e_piece[4]) + e_piece[3]).astype(BF)
    e_acts = dot(e_two, e_units)
    e_gate_act = e_acts[:, :unit]
    e_lift_act = e_acts[:, unit:]
    e_hidden = (jax.nn.silu(e_gate_act) * e_lift_act).astype(BF)
    e_lowered = noise.scatter_sum(token_blocks(dot(e_hidden, e_lower)))

    def own_part(value):
        return lax.dynamic_slice_in_dim(value, noise.me * own_rows, own_rows, 0)

    latent_own = own_part(e_middle) + own_part(e_piece[5]) * e_lowered
    latent_low = latent_own.astype(BF)
    latent_all = jnp.concatenate(noise.gather(latent_low)).astype(F32)

    sines = sinusoid(times, width).astype(BF).reshape(levels * images, width)
    temb = jnp.concatenate(noise.gather(dot(sines, d_time)), -1)
    cond = (
        latent_all.reshape(1, images, length, width)
        + temb.reshape(levels, images, 1, width)
    ).reshape(levels * rows, width)
    cond_low = jax.nn.silu(cond).astype(BF)
    mod = mod_dot(cond_low, d_whole, 6 * quarter)
    shift_one, scale_one, gate_one, shift_two, scale_two, gate_two = [
        mod[n * quarter : (n + 1) * quarter] for n in range(6)
    ]
    ratio = jnp.repeat(times.reshape(-1), length)[None]
    clean_up = lax.dynamic_slice_in_dim(clean_group.T, place, quarter, 0).astype(F32)
    noisy = (1.0 - ratio) * jnp.tile(clean_up, (1, levels)) + ratio * noise_cols.astype(F32)
    norm_one = (noisy - mean_one) * inverse_one
    one = (norm_one * (1.0 + scale_one) + shift_one).astype(BF)
    one_all, heads = join_dot(me, noise.near(one), d_att)
    mixed = attend_forward(heads, decoder_gains, length, True)
    mixed_all, merged = join_dot(me, noise.near(mixed), d_merge, True)
    middle = noisy + gate_one * merged
    part_mean = jnp.mean(middle, 0)
    part_center = middle - part_mean[None]
    part_square = jnp.sum(part_center * part_center, 0)
    parts = noise.near(jnp.stack([part_mean, part_square]))
    mean_two = sum(part[0] for part in parts) / noise_count
    square = sum(part[1] + quarter * (part[0] - mean_two) ** 2 for part in parts)
    inverse_two = lax.rsqrt(square / width + EPS)[None]
    norm_two = (middle - mean_two[None]) * inverse_two
    two = (norm_two * (1.0 + scale_two) + shift_two).astype(BF)
    two_all, acts, hidden = units_dot(me, noise.near(two), d_units)
    lowered = noise.near_sum(*lowered_dot(me, hidden, d_lower))
    output = (middle + gate_two * lowered).astype(BF)
    velocity = jnp.concatenate(
        noise.exchange(jnp.moveaxis(output.reshape(quarter, levels, rows), 1, 0))
    )
    velocity = velocity.T.reshape(1, images, length, width)

    def norm_back_cols(grad, normed, inverse):
        sums = noise.total(jnp.stack([jnp.sum(grad, 0), jnp.sum(grad * normed, 0)]))
        sums = sums[:, None] / width
        return inverse * (grad - sums[0] - normed * sums[1])

    low_cols = (cot_cols * gate_two).astype(BF)
    low_all, g_hidden = lower_back_dot(me, noise.near(low_cols), d_lower)
    g_gate_two = cot_cols * lowered
    g_acts, *given = acts_back(me, g_hidden, acts, d_units, quarter)
    g_two = noise.near_sum(*given)
    gw_lower = grad_dot(hidden, low_all, grad_low_kernel)
    gw_units = grad_dot(two_all, g_acts)
    g_middle = cot_cols + norm_back_cols(g_two * (1.0 + scale_two), norm_two, inverse_two)
    g_merged_low = (g_middle * gate_one).astype(BF)
    g_mixed = noise.near_sum(*spread_up_dot(me, g_merged_low, d_merge))
    gw_merge = grad_dot(mixed_all, g_merged_low, grad_turned_kernel)
    g_heads, d_gain_grad = attend_backward(
        g_mixed.astype(BF), decoder_gains, heads, length, True
    )
    g_one = noise.near_sum(*spread_dot(me, g_heads, d_att))
    gw_att = grad_dot(one_all, g_heads)
    g_noisy = g_middle + norm_back_cols(g_one * (1.0 + scale_one), norm_one, inverse_one)
    g_parts = (
        g_one,
        g_one * norm_one,
        g_middle * merged,
        g_two,
        g_two * norm_two,
        g_gate_two,
    )
    g_mod, g_cond_low = mod_back([part.astype(BF) for part in g_parts], d_whole)
    gw_mod = grad_dot(cond_low, g_mod, grad_low_kernel)
    g_cond = g_cond_low * silu_slope(cond)
    g_temb = noise.scatter_sum(
        column_blocks(jnp.sum(g_cond.reshape(levels * images, length, width), 1)), F32
    ).astype(BF)
    gw_time = dot_tn(sines, g_temb)
    g_latent = noise.scatter_sum(token_blocks(jnp.sum(g_cond.reshape(levels, rows, width), 0)))
    g_clean_cols = jnp.sum(
        ((1.0 - ratio) * g_noisy).reshape(quarter, levels, rows), 1
    ).astype(BF).T
    g_clean = jnp.concatenate(
        noise.exchange(g_clean_cols.reshape(noise_count, own_rows, quarter)), -1
    ).astype(F32)

    piece = [own_part(part) for part in e_piece]
    norm_two_own = own_part(e_norm_two)
    norm_one_own = own_part(e_norm_one)
    e_low_all = jnp.concatenate(noise.gather((g_latent * piece[5]).astype(BF)))
    e_g_gate_two = g_latent * e_lowered
    ew_lower = dot_tn(e_hidden, e_low_all)
    e_g_hidden = dot_nt(e_low_all, e_lower)
    e_g_gate_low = (e_g_hidden * e_lift_act * silu_slope(e_gate_act)).astype(BF)
    e_g_lift_low = (e_g_hidden * jax.nn.silu(e_gate_act)).astype(BF)
    e_g_acts = jnp.concatenate([e_g_gate_low, e_g_lift_low], -1)
    ew_units = dot_tn(e_two, e_g_acts)
    e_g_two = noise.scatter_sum(token_blocks(dot_nt(e_g_acts, e_units)))
    e_g_middle = g_latent + norm_back(
        e_g_two * (1.0 + piece[4]), norm_two_own, own_part(e_inverse_two)
    )
    e_merged_low = jnp.concatenate(noise.gather((e_g_middle * piece[2]).astype(BF)))
    e_merged_cols = columns(e_merged_low)
    ew_merge = dot_tn(e_mixed_all, e_merged_cols)
    e_g_mixed = noise.scatter_sum(column_blocks(dot_nt(e_merged_cols, e_merge)))
    e_g_heads, e_gain_grad = attend_backward(
        e_g_mixed.astype(BF), encoder_gains, e_heads, length
    )
    ew_att = dot_tn(e_one, e_g_heads)
    e_g_one = noise.scatter_sum(token_blocks(dot_nt(e_g_heads, e_att)))
    e_g_clean = e_g_middle + norm_back(
        e_g_one * (1.0 + piece[1]), norm_one_own, own_part(e_inverse_one)
    )
    clean_grad = (e_g_clean + g_clean).reshape(own_images, length, width)
    e_g_mod = jnp.concatenate(
        [
            e_g_one,
            e_g_one * norm_one_own,
            e_g_middle * own_part(e_merged),
            e_g_two,
            e_g_two * norm_two_own,
            e_g_gate_two,
        ],
        -1,
    )
    e_g_mod = jnp.sum(e_g_mod.reshape(own_images, length, -1), 1).astype(BF)
    every_mod = noise.exchange(
        jnp.moveaxis(e_g_mod.reshape(own_images, noise_count, -1), 1, 0)
    )
    every_mod = jnp.concatenate(every_mod)
    gains = noise.total(jnp.stack([e_gain_grad, d_gain_grad]))
    message = jnp.concatenate([every_mod.astype(F32).reshape(-1), gains.reshape(-1)])
    message = groups.gather_direct(message)
    every_mod, gain_total = message[:, : every_mod.size], message[:, every_mod.size :]
    every_mod = every_mod.astype(BF).reshape(-1, encoder_modulate.shape[1])
    gain_total = jnp.sum(gain_total, 0).reshape(gains.shape)
    grad_e_mod = dot_tn(class_low, every_mod)
    g_class = noise.total(dot_nt(every_mod, encoder_modulate)) * silu_slope(class_cond)
    grad_table = lax.dot_general(
        g_class,
        onehot.astype(F32),
        (((0,), (0,)), ((), ())),
        precision=lax.Precision.HIGHEST,
        preferred_element_type=F32,
    )

    def by_group(grad):
        low = grad.astype(BF)
        return low.reshape((groups_count, -1) + low.shape[1:])

    def finish_pieces(mine, pieces):
        mine = mine.astype(BF).reshape(mine.shape[0], pieces, quarter)
        came = jnp.stack(noise.exchange(return_pieces(noise, mine)))
        return join_pieces(noise, came, pieces).astype(F32)

    def finish_units(mine):
        came = jnp.stack(noise.exchange(return_units(noise, mine.astype(BF))))
        return join_units(noise, groups, came).astype(F32)

    def finish_lower(mine):
        mine = mine.astype(BF).reshape(-1, width)
        came = jnp.stack(noise.exchange(column_blocks(mine)))
        return came.reshape(-1, quarter).astype(F32)

    def finish(arrays, picked, e_or_d):
        kinds = tuple(e_or_d[n] for n in picked)
        full = (
            (chunk_rows, encoder_attend.shape[1]),
            (chunk_rows, unit),
            (chunk_rows, unit),
            encoder_lower.shape,
            (chunk_rows, encoder_modulate.shape[1]),
        )
        if groups.quick:
            return trade(
                noise,
                me,
                arrays,
                kinds,
                low_units,
                True,
                [full[n] for n in picked],
                F32,
            )
        ends = {"units": finish_units, "lower": finish_lower}
        return [
            finish_pieces(array, kind[1]) if kind[0] == "pieces" else ends[kind[0]](array)
            for array, kind in zip(arrays, kinds)
        ]

    d_second = groups.sum_whole(
        jnp.concatenate([by_group(gw_units), pad_lower(by_group(gw_lower))], 1)
    )
    grad_d_gate, grad_d_lift, grad_d_lower = finish(
        (
            d_second[:chunk_rows, :unit],
            d_second[:chunk_rows, unit:],
            d_second[chunk_rows:, :width],
        ),
        (1, 2, 3),
        d_kinds,
    )
    d_first = groups.sum_whole(
        jnp.concatenate([by_group(part) for part in [gw_mod, gw_att, gw_merge, gw_time]], -1)
    )
    grad_d_att, grad_d_mod = finish(
        (d_first[:, 6 * quarter : 9 * quarter], d_first[:, : 6 * quarter]), (0, 4), d_kinds
    )
    grad_d_merge = d_first[:, 9 * quarter : 10 * quarter]
    grad_time = d_first[:, 10 * quarter :]
    e_low_sum = groups.scatter_sum(by_group(ew_lower))
    e_second = groups.scatter_sum(
        by_group(ew_units)
    )
    e_first = groups.scatter_sum(
        jnp.concatenate([by_group(part) for part in [ew_att, ew_merge]], -1)
    )
    grad_e_att, grad_e_gate, grad_e_lift, grad_e_lower = finish(
        (e_first[:, : 3 * quarter], e_second[:, :unit], e_second[:, unit:], e_low_sum),
        (0, 1, 2, 3),
        e_kinds,
    )
    grad_e_merge = e_first[:, 3 * quarter :]
    return (
        velocity,
        latent_low.reshape(own_images, length, width),
        clean_grad,
        grad_e_mod,
        grad_e_att,
        grad_e_merge,
        grad_e_gate,
        grad_e_lift,
        grad_e_lower,
        grad_table,
        gain_total[0],
        grad_d_mod,
        grad_d_att,
        grad_d_merge,
        grad_d_gate,
        grad_d_lift,
        grad_d_lower,
        grad_time,
        gain_total[1],
    )


def solution(mesh):
    return jax.shard_map(
        functools.partial(per_device, mesh.shape["dp"], mesh.shape["noise"]),
        mesh=mesh,
        in_specs=(
            P(("dp", "noise"), None, None),
            P("noise", "dp", None, None),
            P("noise", "dp"),
            P(("dp", "noise")),
            P("noise", "dp", None, None),
            P("dp", "noise"),
            P("dp", "noise"),
            P("dp", "noise"),
            P("dp", "noise"),
            P("dp", "noise"),
            P("dp", "noise"),
            P("dp", "noise"),
            P(),
            P("dp", "noise"),
            P("dp", "noise"),
            P("dp", "noise"),
            P("dp", "noise"),
            P("dp", "noise"),
            P("dp", "noise"),
            P("dp", "noise"),
            P(),
        ),
        out_specs=(
            P("noise", "dp", None, None),
            P(("dp", "noise"), None, None),
            P(("dp", "noise"), None, None),
            P("dp", "noise"),
            P("dp", "noise"),
            P("dp", "noise"),
            P("dp", "noise"),
            P("dp", "noise"),
            P("dp", "noise"),
            P("dp", "noise"),
            P(),
            P("dp", "noise"),
            P("dp", "noise"),
            P("dp", "noise"),
            P("dp", "noise"),
            P("dp", "noise"),
            P("dp", "noise"),
            P("dp", "noise"),
            P(),
        ),
        check_vma=False,
    )
```
